32 devices in a mesh: slab: 16 (over z, y, core), tp: 2 (over x).
Axes of the slice: x: 2, y: 2, z: 4, core: 2. Of those that a mesh axis runs over, the one named last changes fastest.
Arguments:
- tokens: bfloat16 [4096, 768], P(('slab', 'tp')), may hold values from -6 to 6
- mask_index: int32 [2457], replicated, may hold values from 0 to 4095, as said below
- mask_token: bfloat16 [768], replicated, may hold values from -6 to 6
- norm_gain: float32 [768], replicated, may hold values from 0.5 to 2
- w_in: bfloat16 [768, 3072], P(None, 'tp'), may hold values from -0.21875 to 0.21875
- b_in: float32 [3072], P('tp'), may hold values from -3 to 3
- w_out: bfloat16 [3072, 768], P('tp'), may hold values from -0.109375 to 0.109375
- b_out: float32 [768], replicated, may hold values from -3 to 3
- w_up: bfloat16 [768, 3072], replicated, may hold values from -0.21875 to 0.21875
- b_up: float32 [384], replicated, may hold values from -3 to 3
- skip: bfloat16 [32, 16, 64, 384], P('slab', 'tp'), may hold values from -6 to 6
- w_conv: bfloat16 [27, 384, 384], P(None, 'slab'), may hold values from -0.0625 to 0.0625
- b_conv: float32 [384], replicated, may hold values from -3 to 3
Outputs:
- features: bfloat16 [32, 16, 64, 384], P('slab', 'tp')
The draws below stay inside these ranges and needn't reach their ends.
Inputs may be any that keep to these rules, and one draw needn't show every extreme that they name: `mask_index`: 2457 distinct token indices.
All inputs are finite; a program needn't handle non-finite values.
Results may differ from the reference program's by a relative error of at most 0.013.
Values may be sent and summed in bfloat16 or wider, within the bound.
No kernel may reach another device: no remote copies, remote signals or barrier semaphores. Data moves between devices by JAX's collectives and lax.ppermute only.
A program may use at most 128 MiB of HBM per device.

```python
import math
import jax
import jax.numpy as jnp
from jax import lax

D = 768
HID = 3072
C = 384
BX = 32
BZ = 16
BY = 8
TOKENS = 4096
MASKED = 2457
NZ = 32
NY = 16
NX = 64


def draw_mask_index(key, part):
    middle = jax.random.permutation(key, TOKENS - 2)[:MASKED - 2] + 1
    ends = jnp.array([0, TOKENS - 1], jnp.int32)
    return jnp.concatenate([ends, middle.astype(jnp.int32)]).astype(jnp.int32)


def steps_of(stream_key, extent, split, smallest, high):
    def one(axis_at, blocks):
        steps = jax.random.uniform(jax.random.fold_in(jax.random.fold_in(stream_key, 6), axis_at), (blocks,), jnp.float32, smallest / len(split), high / len(split))
        return jnp.repeat(jnp.exp(steps), extent[axis_at] // blocks).reshape((-1,) + (1,) * (len(extent) - axis_at - 1))

    factor_of = one(*split[0])
    for cut in split[1:]:
        factor_of = factor_of * one(*cut)
    return factor_of


def normal_values(stream_key, shape, scale, limit, shards=(), dtype=jnp.bfloat16):
    entries = jax.random.normal(stream_key, shape, jnp.float32) * scale
    if len(shards) > 0:
        entries = steps_of(stream_key, shape, shards, -0.22, 0.18) * entries
    return jnp.clip(entries, min=-limit, max=limit).astype(dtype)


def setup_inputs(seed: int = 0) -> dict:
    streams_of = jax.random.split(jax.random.key(seed), 14)
    return {
        "tokens": normal_values(streams_of[0], (TOKENS, D), 1.0, 6.0, ((0, 32),)),
        "mask_index": draw_mask_index(jax.random.fold_in(streams_of[13], 71), 0),
        "mask_token": normal_values(streams_of[2], (D,), 1.0, 6.0),
        "norm_gain": jnp.clip(jnp.exp(jax.random.uniform(streams_of[3], (D,), jnp.float32, math.log(0.5), math.log(2.0))), 0.5, 2.0),
        "w_in": normal_values(streams_of[4], (D, HID), D ** -0.5, 0.21875, ((1, 2),)),
        "b_in": normal_values(streams_of[5], (HID,), 0.5, 3.0, ((0, 2),), jnp.float32),
        "w_out": normal_values(streams_of[6], (HID, D), HID ** -0.5, 0.109375, ((0, 2),)),
        "b_out": normal_values(streams_of[7], (D,), 0.5, 3.0, (), jnp.float32),
        "w_up": normal_values(streams_of[8], (D, 8 * C), D ** -0.5, 0.21875),
        "b_up": normal_values(streams_of[9], (C,), 0.5, 3.0, (), jnp.float32),
        "skip": normal_values(streams_of[10], (NZ, NY, NX, C), 1.0, 6.0, ((0, 16), (1, 2))),
        "w_conv": normal_values(streams_of[11], (27, C, C), (27 * C) ** -0.5, 0.0625, ((1, 16),)),
        "b_conv": normal_values(streams_of[12], (C,), 0.5, 3.0, (), jnp.float32),
    }


def reference(tokens, mask_index, mask_token, norm_gain, w_in, b_in, w_out, b_out, w_up, b_up, skip, w_conv, b_conv):
    flags = jnp.zeros((TOKENS,), jnp.float32).at[mask_index].set(1.0)
    filled = jnp.where(flags[:, None] > 0.5, mask_token[None, :], tokens)
    values = filled.astype(jnp.float32)
    mean = lax.optimization_barrier(jnp.mean(values, axis=1, keepdims=True))
    var = lax.optimization_barrier(jnp.mean((values - mean) ** 2, axis=1, keepdims=True))
    normed = ((values - mean) * lax.rsqrt(var + 1e-05) * norm_gain).astype(jnp.bfloat16)
    hidden = jax.nn.gelu(jnp.dot(normed, w_in, preferred_element_type=jnp.float32) + b_in, approximate=False).astype(jnp.bfloat16)
    bottleneck = (values + jnp.dot(hidden, w_out, preferred_element_type=jnp.float32) + b_out).astype(jnp.bfloat16)
    upward = jnp.dot(bottleneck, w_up, preferred_element_type=jnp.float32)
    upward = upward.reshape(BZ, BY, BX, 2, 2, 2, C).transpose(0, 3, 1, 4, 2, 5, 6).reshape(NZ, NY, NX, C)
    upsampled = (upward + b_up + skip.astype(jnp.float32)).astype(jnp.bfloat16)
    kernel = w_conv.astype(jnp.float32).reshape(3, 3, 3, C, C)
    conv = lax.conv_general_dilated(upsampled.astype(jnp.float32)[None], kernel, (1, 1, 1), [(1, 1), (1, 1), (1, 1)], dimension_numbers=('NDHWC', 'DHWIO', 'NDHWC'), precision=lax.Precision.HIGHEST)[0]
    summed = conv + b_conv
    return jnp.where(summed > 0, summed, 0.01 * summed).astype(jnp.bfloat16)
```

```python
import functools
import math

import jax
import jax.numpy as jnp
from jax import lax
from jax.experimental import pallas as pl
from jax.experimental.pallas import tpu as pltpu
from jax.sharding import PartitionSpec as P

BF = jnp.bfloat16
F32 = jnp.float32
BX = 32
VMEM_LIMIT = 56 * 1024 * 1024


def in_vmem(*_):
    return pl.BlockSpec(memory_space=pltpu.VMEM)


def in_smem(*_):
    return pl.BlockSpec(memory_space=pltpu.SMEM)


def mlp_kernel(count, rows, info_ref, mask_ref, mtok_ref, gain_ref, bout_ref, bin_ref, *refs):
    toks = refs[:count]
    w_in_ref, w_out_ref = refs[count : count + 2]
    base_ref = refs[count + 2]
    sends = refs[count + 3 : 2 * count + 2]
    normed_ref, filled_ref, acc_ref = refs[2 * count + 2 :]
    step = pl.program_id(0)

    @pl.when(step == 0)
    def _():
        index = mask_ref[...]
        for k in range(count):
            ids = lax.broadcasted_iota(jnp.int32, (rows, 1), 0) + info_ref[k]
            hit = jnp.where(index == ids, 1.0, 0.0)
            flag = jnp.max(hit, axis=1, keepdims=True)
            tok = toks[k][0:rows, :].astype(F32)
            values = jnp.where(flag > 0.5, mtok_ref[...].astype(F32), tok)
            mean = jnp.mean(values, axis=1, keepdims=True)
            cent = values - mean
            var = jnp.mean(cent * cent, axis=1, keepdims=True)
            normed = cent * lax.rsqrt(var + 1e-05) * gain_ref[...]
            normed_ref[k * rows : (k + 1) * rows, :] = normed.astype(BF)
            filled_ref[k * rows : (k + 1) * rows, :] = values
        acc_ref[...] = jnp.zeros_like(acc_ref)

    pre = jnp.dot(normed_ref[...], w_in_ref[...], preferred_element_type=F32) + bin_ref[...]
    hidden = (0.5 * pre * (1.0 + lax.erf(pre * math.sqrt(0.5)))).astype(BF)
    acc_ref[...] += jnp.dot(hidden, w_out_ref[...], preferred_element_type=F32)

    @pl.when(step == pl.num_programs(0) - 1)
    def _():
        for k in range(count):
            parts = [(pl.ds(k * rows, rows), 0, rows)]
            at = rows
            if count == 2:
                other = ((k + 1) % 2) * rows
                start = other + jnp.where(info_ref[count + k] == 0, 0, rows - BX)
                parts.append((pl.ds(pl.multiple_of(start, BX), BX), at, BX))
            else:
                low = ((k - 1) % count) * rows + rows - BX
                high = ((k + 1) % count) * rows
                parts.append((pl.ds(low, BX), at, BX))
                parts.append((pl.ds(high, BX), at + BX, BX))
            for src, dst, size in parts:
                if k == 0:
                    base_ref[dst : dst + size, :] = acc_ref[src, :] + filled_ref[src, :] + bout_ref[...]
                else:
                    sends[k - 1][dst : dst + size, :] = acc_ref[src, :].astype(BF)


def mlp(tokens, peers, mask_index, mask_token, norm_gain, w_in, b_in, w_out, b_out, info):
    count = len(peers) + 1
    rows, width = tokens.shape
    hidden = w_in.shape[1]
    chunk = next(c for c in (256, 128, hidden) if hidden % c == 0)
    slots = 1 if count == 2 else 2
    total = rows + slots * BX
    fixed = lambda *shape: pl.BlockSpec(shape, lambda j: (0,) * len(shape))
    outs = [jax.ShapeDtypeStruct((total, width), F32)] + [
        jax.ShapeDtypeStruct((total, width), BF) for _ in peers
    ]
    return pl.pallas_call(
        functools.partial(mlp_kernel, count, rows),
        grid=(hidden // chunk,),
        in_specs=[
            in_smem(),
            fixed(1, mask_index.shape[0]),
            fixed(1, width),
            fixed(1, width),
            fixed(1, width),
            pl.BlockSpec((1, chunk), lambda j: (0, j)),
            fixed(rows, width),
            *[fixed(*p.shape) for p in peers],
            pl.BlockSpec((width, chunk), lambda j: (0, j)),
            pl.BlockSpec((chunk, width), lambda j: (j, 0)),
        ],
        out_specs=[fixed(total, width) for _ in outs],
        out_shape=outs,
        scratch_shapes=[
            pltpu.VMEM((count * rows, width), BF),
            pltpu.VMEM((count * rows, width), F32),
            pltpu.VMEM((count * rows, width), F32),
        ],
        compiler_params=pltpu.CompilerParams(vmem_limit_bytes=VMEM_LIMIT),
        cost_estimate=pl.CostEstimate(
            flops=4 * count * rows * width * hidden,
            bytes_accessed=4 * width * hidden,
            transcendentals=count * rows * hidden,
        ),
        name="mlp",
    )(
        info,
        mask_index.reshape(1, -1),
        mask_token.reshape(1, -1),
        norm_gain.reshape(1, -1),
        b_out.reshape(1, -1),
        b_in.reshape(1, -1),
        tokens,
        *peers,
        w_in,
        w_out,
    )


def up_kernel(count, rows, arrived, info_ref, base_ref, *refs):
    recvs = refs[:arrived]
    w_ref, bup_ref, skip_ref, edge_ref, out_ref, bott_ref, wide_ref = refs[arrived:]
    b = pl.program_id(0)
    channels = bup_ref.shape[1]
    slots = edge_ref.shape[0]
    y_rows = rows // BX
    last = out_ref.shape[0] - 1

    @pl.when(b == 0)
    def _():
        total = base_ref[...]
        for r in recvs:
            total = total + r[...].astype(F32)
        bott_ref[...] = total.astype(BF)

    up = jnp.dot(bott_ref[...], w_ref[...], preferred_element_type=F32)
    size = up.shape[0]
    for c in range(2):
        for l in range(0, channels, 128):
            wide_ref[l // 128, pl.ds(c, size, stride=2), :] = up[:, c * channels + l : c * channels + l + 128]
    bias = bup_ref[...]

    def fine_row(at):
        return jnp.concatenate(
            [wide_ref[l // 128, at * 2 * BX : (at + 1) * 2 * BX, :] for l in range(0, channels, 128)], axis=1
        )

    for y in range(y_rows):
        row = fine_row(y) + bias + skip_ref[0, 2 * y + b].astype(F32)
        out_ref[1 + 2 * y + b] = row.astype(BF)
    me = info_ref[1]
    if count == 2:
        value = (fine_row(y_rows) + bias + edge_ref[0].astype(F32)).astype(BF)
        low = me == 1

        @pl.when(b == jnp.where(low, 1, 0))
        def _():
            out_ref[jnp.where(low, 0, last)] = value
            out_ref[jnp.where(low, last, 0)] = jnp.zeros_like(value)

    else:
        for slot in range(2):
            ok = (me > 0) if slot == 0 else (me < count - 1)
            value = fine_row(y_rows + slot) + bias + edge_ref[slot].astype(F32)
            value = jnp.where(ok, value, 0.0).astype(BF)

            @pl.when(b == 1 - slot)
            def _(value=value, slot=slot):
                out_ref[0 if slot == 0 else last] = value


def upsample(count, rows, base, recvs, w_up, b_up, skip, edge, info):
    channels = b_up.shape[0]
    y_len, x_len = skip.shape[1:3]
    slots = edge.shape[1]
    total, width = base.shape
    fixed = lambda *shape: pl.BlockSpec(shape, lambda b, info: (0,) * len(shape))
    return pl.pallas_call(
        functools.partial(up_kernel, count, rows, len(recvs)),
        grid_spec=pltpu.PrefetchScalarGridSpec(
            num_scalar_prefetch=1,
            grid=(2,),
            in_specs=[
                fixed(total, width),
                *[fixed(total, width) for _ in recvs],
                pl.BlockSpec((width, 2 * channels), lambda b, info: (0, 2 * info[0] + b)),
                fixed(1, channels),
                pl.BlockSpec((1, y_len, x_len, channels), lambda b, info: (info[0], 0, 0, 0)),
                pl.BlockSpec((None, slots, x_len, channels), lambda b, info: (info[0], 0, 0, 0)),
            ],
            out_specs=fixed(y_len + 2, x_len, channels),
            scratch_shapes=[
                pltpu.VMEM((total, width), BF),
                pltpu.VMEM((channels // 128, 2 * total, 128), F32),
            ],
        ),
        out_shape=jax.ShapeDtypeStruct((y_len + 2, x_len, channels), BF),
        compiler_params=pltpu.CompilerParams(vmem_limit_bytes=VMEM_LIMIT),
        cost_estimate=pl.CostEstimate(
            flops=8 * total * width * channels,
            bytes_accessed=8 * width * channels,
            transcendentals=0,
        ),
        name="upsample",
    )(info, base, *recvs, w_up, b_up.reshape(1, -1), skip, edge)


def conv_kernel(layout, cut, info_ref, *refs):
    planes = refs[:4]
    pieces = refs[4 : 4 + len(layout)]
    bias_ref, out_ref, w_ref, sem = refs[4 + len(layout) :]
    core = info_ref[0]
    band = pieces[0].shape[1]
    taps = pieces[0].shape[0]
    copies = []
    for n, (piece, (slot, flip)) in enumerate(zip(pieces, layout)):
        second = (core + flip) % 2
        at = pl.multiple_of(info_ref[1 + slot] * band, math.gcd(band, 16))
        copy = pltpu.make_async_copy(
            piece, w_ref.at[pl.ds(second * taps, taps), pl.ds(at, band), :], sem.at[n]
        )
        copy.start()
        copies.append(copy)
    for copy in copies:
        copy.wait()

    y_len, x_len, channels = out_ref.shape[1:]
    size = y_len * x_len
    at_x = lax.broadcasted_iota(jnp.int32, (size, 1), 0) % x_len
    for j in range(2):
        lhs = jnp.concatenate(
            [planes[j + dz][dy : dy + y_len].reshape(size, channels) for dz in range(3) for dy in range(3)],
            axis=1,
        )
        total = None
        for dx in range(3):
            rows = []
            for dz in range(3):
                true_dz = jnp.where(core == 0, dz, 2 - dz)
                for dy in range(3):
                    tap = 9 * true_dz + 3 * dy + dx
                    rows.append(w_ref[tap + jnp.where(tap > cut, 2 * taps - 27, 0)])
            part = jnp.dot(lhs, jnp.concatenate(rows, axis=0), preferred_element_type=F32)
            if dx == 0:
                part = jnp.where(at_x == 0, 0.0, pltpu.roll(part, 1, 0))
            if dx == 2:
                part = jnp.where(at_x == x_len - 1, 0.0, pltpu.roll(part, size - 1, 0))
            total = part if total is None else total + part
        total = total + bias_ref[...]
        total = jnp.where(total > 0, total, 0.01 * total)
        out_ref[jnp.where(core == 0, j, 1 - j)] = total.astype(BF).reshape(y_len, x_len, channels)


def convolve(planes, pieces, layout, b_conv, info, y_len):
    taps, band, channels = pieces[0].shape
    cut = 26 - taps
    x_len = planes[0].shape[1]
    return pl.pallas_call(
        functools.partial(conv_kernel, layout, cut),
        in_specs=[
            in_smem(),
            *[in_vmem() for _ in planes],
            *[pl.BlockSpec(memory_space=pl.ANY) for _ in pieces],
            in_vmem(),
        ],
        out_specs=in_vmem(),
        out_shape=jax.ShapeDtypeStruct((2, y_len, x_len, channels), BF),
        scratch_shapes=[
            pltpu.VMEM((2 * taps, channels, channels), BF),
            pltpu.SemaphoreType.DMA((len(pieces),)),
        ],
        compiler_params=pltpu.CompilerParams(vmem_limit_bytes=VMEM_LIMIT),
        cost_estimate=pl.CostEstimate(
            flops=2 * 2 * y_len * x_len * 27 * channels * channels,
            bytes_accessed=27 * channels * channels * 2,
            transcendentals=0,
        ),
        name="conv",
    )(info, *planes, *pieces, b_conv.reshape(1, -1))


def gather_kernel_pieces(w_conv, slabs, core):
    chips = slabs // 2
    order = list(range(0, chips, 2)) + list(range(chips - 1, 0, -2))
    mates = [(s, s ^ 1) for s in range(slabs)]
    ring = []
    for at in range(chips):
        ring.append((2 * order[at], 2 * order[(at + 1) % chips]))
        ring.append((2 * order[at] + 1, 2 * order[(at - 1) % chips] + 1))
    position = jnp.asarray([order.index(chip) for chip in range(chips)], jnp.int32)
    chip_at = jnp.asarray(order, jnp.int32)
    here = position[lax.axis_index("slab") // 2]
    sign = 1 - 2 * core

    taps = (w_conv.shape[0] + 1) // 2
    if (2 * w_conv.shape[1]) % 16:
        whole = lax.all_gather(w_conv, "slab", axis=1, tiled=True)
        low, high = whole[:taps], whole[w_conv.shape[0] - taps :]
        return (
            [jnp.where(core == 0, low, high), jnp.where(core == 0, high, low)],
            [(0, 0), (0, 1)],
            [jnp.int32(0)],
        )
    mate = lax.ppermute(w_conv, "slab", mates)
    first_core = core == 0
    unit = jnp.concatenate(
        [jnp.where(first_core, w_conv, mate), jnp.where(first_core, mate, w_conv)], axis=1
    )
    low, high = unit[:taps], unit[w_conv.shape[0] - taps :]
    first = jnp.where(first_core, low, high)
    second = jnp.where(first_core, high, low)
    pieces, layout, chip_list = [first, second], [(0, 0), (0, 1)], [lax.axis_index("slab") // 2]
    a, b = first, second
    for k in range(1, chips // 2 + 1):
        final = 2 * k == chips
        mine = chip_at[(here - sign * k) % chips]
        theirs = chip_at[(here + sign * k) % chips]
        chip_list += [mine, theirs]
        slot = len(chip_list) - 2
        a = lax.ppermute(a, "slab", ring)
        pieces.append(a)
        layout.append((slot, 0))
        pieces.append(lax.ppermute(a, "slab", mates))
        layout.append((slot + 1, 1))
        if not final:
            b = lax.ppermute(b, "slab", ring)
            pieces.append(b)
            layout.append((slot, 1))
            pieces.append(lax.ppermute(b, "slab", mates))
            layout.append((slot + 1, 0))
    return pieces, layout, chip_list


def on_device(
    tokens,
    mask_index,
    mask_token,
    norm_gain,
    w_in,
    b_in,
    w_out,
    b_out,
    w_up,
    b_up,
    skip,
    w_conv,
    b_conv,
):
    count = lax.axis_size("tp")
    slabs = lax.axis_size("slab")
    me = lax.axis_index("tp")
    slab = lax.axis_index("slab")
    core = slab % 2
    rows, width = tokens.shape
    y_len, x_len, channels = skip.shape[1:]

    def from_peer(k):
        return [((i + k) % count, i) for i in range(count)]

    if count == 2:
        edge = lax.dynamic_index_in_dim(skip, jnp.where(me == 0, y_len - 1, 0), axis=1, keepdims=False)
        packed = jnp.concatenate([tokens, jnp.concatenate([edge[0], edge[1]], axis=1)], axis=0)
        packed = lax.ppermute(packed, "tp", from_peer(1))
        peers = [packed]
        edge = packed[rows:].reshape(x_len, 2, 1, channels).transpose(1, 2, 0, 3)
    else:
        peers = [lax.ppermute(tokens, "tp", from_peer(k)) for k in range(1, count)]
        low = lax.ppermute(skip[:, y_len - 1], "tp", [(i, i + 1) for i in range(count - 1)])
        high = lax.ppermute(skip[:, 0], "tp", [(i + 1, i) for i in range(count - 1)])
        edge = jnp.stack([low, high], axis=1)

    pieces, layout, chip_list = gather_kernel_pieces(w_conv, slabs, core)

    ranks = [(me + k) % count for k in range(count)]
    mlp_info = jnp.stack([(slab * count + r) * rows for r in ranks] + ranks).astype(jnp.int32)
    base, *sends = mlp(
        tokens, peers, mask_index, mask_token, norm_gain, w_in, b_in, w_out, b_out, mlp_info
    )
    recvs = [
        lax.ppermute(s, "tp", [(i, (i + k) % count) for i in range(count)])
        for k, s in enumerate(sends, start=1)
    ]

    up = functools.partial(upsample, count, rows, base, recvs, w_up, b_up, skip, edge)
    outer = up(jnp.stack([core, me]).astype(jnp.int32))
    beyond = lax.ppermute(
        outer,
        "slab",
        [(s, s + 1) for s in range(1, slabs - 1, 2)] + [(s + 1, s) for s in range(1, slabs - 1, 2)],
    )
    inner = up(jnp.stack([1 - core, me]).astype(jnp.int32))
    mates = lax.ppermute(inner, "slab", [(s, s ^ 1) for s in range(slabs)])

    conv_info = jnp.stack([core] + chip_list).astype(jnp.int32)
    return convolve([beyond, outer, inner, mates], pieces, layout, b_conv, conv_info, y_len)


def solution(mesh):
    in_specs = (
        P(("slab", "tp"), None),
        P(),
        P(),
        P(),
        P(None, "tp"),
        P("tp"),
        P("tp", None),
        P(),
        P(),
        P(),
        P("slab", "tp", None, None),
        P(None, "slab", None),
        P(),
    )
    out_specs = P("slab", "tp", None, None)
    return jax.shard_map(
        on_device, mesh=mesh, in_specs=in_specs, out_specs=out_specs, check_vma=False
    )
```

```python
import functools
import math

import jax
import jax.numpy as jnp
from jax import lax
from jax.experimental import pallas as pl
from jax.experimental.pallas import tpu as pltpu
from jax.sharding import PartitionSpec as P

BF = jnp.bfloat16
F32 = jnp.float32
BX = 32
VMEM_LIMIT = 56 * 1024 * 1024


def in_vmem(*_):
    return pl.BlockSpec(memory_space=pltpu.VMEM)


def in_smem(*_):
    return pl.BlockSpec(memory_space=pltpu.SMEM)


def mlp_kernel(count, rows, chunk, mask_ref, mtok_ref, gain_ref, bout_ref, bin_ref, *refs):
    toks = refs[:count]
    w_in_ref, w_out_ref = refs[count : count + 2]
    base_ref = refs[count + 2]
    sends = refs[count + 3 : 2 * count + 2]
    normed_ref, filled_ref, acc_ref = refs[2 * count + 2 :]
    me = lax.axis_index("tp")
    plane = lax.axis_index("slab") * (count * rows)

    index = mask_ref[...][None, :]
    mask_token = mtok_ref[...].astype(F32)[None, :]
    gain = gain_ref[...][None, :]
    for k in range(count):
        first = plane + lax.rem(me + k, count) * rows
        ids = lax.broadcasted_iota(jnp.int32, (rows, 1), 0) + first
        hit = jnp.where(index == ids, 1.0, 0.0)
        flag = jnp.max(hit, axis=1, keepdims=True)
        values = jnp.where(flag > 0.5, mask_token, toks[k][0:rows, :].astype(F32))
        mean = jnp.mean(values, axis=1, keepdims=True)
        cent = values - mean
        var = jnp.mean(cent * cent, axis=1, keepdims=True)
        normed = cent * lax.rsqrt(var + 1e-05) * gain
        normed_ref[k * rows : (k + 1) * rows, :] = normed.astype(BF)
        filled_ref[k * rows : (k + 1) * rows, :] = values

    hidden_size = w_in_ref.shape[1]
    for at in range(0, hidden_size, chunk):
        pre = jnp.dot(normed_ref[...], w_in_ref[:, at : at + chunk], preferred_element_type=F32)
        pre = pre + bin_ref[at : at + chunk][None, :]
        hidden = (0.5 * pre * (1.0 + lax.erf(pre * math.sqrt(0.5)))).astype(BF)
        part = jnp.dot(hidden, w_out_ref[at : at + chunk, :], preferred_element_type=F32)
        if at == 0:
            acc_ref[...] = part
        else:
            acc_ref[...] += part

    bout = bout_ref[...][None, :]
    for k in range(count):
        parts = [(pl.ds(k * rows, rows), 0, rows)]
        if count == 2:
            low = lax.rem(me + k, count) == 0
            start = ((k + 1) % 2) * rows + jnp.where(low, 0, rows - BX)
            parts.append((pl.ds(pl.multiple_of(start, BX), BX), rows, BX))
        else:
            parts.append((pl.ds(((k - 1) % count) * rows + rows - BX, BX), rows, BX))
            parts.append((pl.ds(((k + 1) % count) * rows, BX), rows + BX, BX))
        for src, dst, size in parts:
            if k == 0:
                base_ref[dst : dst + size, :] = acc_ref[src, :] + filled_ref[src, :] + bout
            else:
                sends[k - 1][dst : dst + size, :] = acc_ref[src, :].astype(BF)


def mlp(tokens, peers, mask_index, mask_token, norm_gain, w_in, b_in, w_out, b_out):
    count = len(peers) + 1
    rows, width = tokens.shape
    hidden = w_in.shape[1]
    chunk = next(c for c in (256, 128, hidden) if hidden % c == 0)
    total = rows + (1 if count == 2 else 2) * BX
    outs = [jax.ShapeDtypeStruct((total, width), F32)] + [
        jax.ShapeDtypeStruct((total, width), BF) for _ in peers
    ]
    return pl.pallas_call(
        functools.partial(mlp_kernel, count, rows, chunk),
        in_specs=[in_vmem() for _ in range(8 + len(peers))],
        out_specs=[in_vmem() for _ in outs],
        out_shape=outs,
        scratch_shapes=[
            pltpu.VMEM((count * rows, width), BF),
            pltpu.VMEM((count * rows, width), F32),
            pltpu.VMEM((count * rows, width), F32),
        ],
        compiler_params=pltpu.CompilerParams(vmem_limit_bytes=VMEM_LIMIT),
        cost_estimate=pl.CostEstimate(
            flops=4 * count * rows * width * hidden,
            bytes_accessed=4 * width * hidden,
            transcendentals=count * rows * hidden,
        ),
        name="mlp",
    )(mask_index, mask_token, norm_gain, b_out, b_in, tokens, *peers, w_in, w_out)


def up_kernel(count, rows, outer, arrived, first, base_ref, *refs):
    recvs = refs[:arrived]
    edges = refs[arrived : arrived + (1 if count == 2 else 2)]
    w_ref, bup_ref, skip_ref, out_ref, bott_ref, wide_ref = refs[arrived + len(edges) :]
    core = lax.rem(lax.axis_index("slab"), 2)
    me = lax.axis_index("tp")
    a = core if outer else 1 - core
    channels = bup_ref.shape[0]
    y_rows = rows // BX
    last = out_ref.shape[0] - 1
    bias = bup_ref[...][None, :]

    total = base_ref[...]
    for r in recvs:
        total = total + r[...].astype(F32)
    bott_ref[...] = total.astype(BF)
    size = total.shape[0]
    mine = pl.ds(pl.multiple_of(a * channels, 128), channels)

    for b in range(2):
        start = pl.multiple_of((4 * a + 2 * b) * channels, 128)
        up = jnp.dot(bott_ref[...], w_ref[:, pl.ds(start, 2 * channels)], preferred_element_type=F32)
        for c in range(2):
            for l in range(0, channels, 128):
                wide_ref[b, l // 128, pl.ds(c, size, stride=2), :] = up[
                    :, c * channels + l : c * channels + l + 128
                ]

        def fine_row(at):
            return jnp.concatenate(
                [
                    wide_ref[b, l // 128, at * 2 * BX : (at + 1) * 2 * BX, :]
                    for l in range(0, channels, 128)
                ],
                axis=1,
            )

        for y in range(y_rows):
            row = fine_row(y) + bias + skip_ref[a, 2 * y + b].astype(F32)
            out_ref[1 + 2 * y + b] = row.astype(BF)
        if count == 2:
            value = fine_row(y_rows) + bias + edges[0][first:, mine].astype(F32)
            used = me == b
            out_ref[last if b == 0 else 0] = jnp.where(used, value, 0.0).astype(BF)
        else:
            slot = 1 - b
            ok = (me > 0) if slot == 0 else (me < count - 1)
            value = fine_row(y_rows + slot) + bias + edges[slot][first:, mine].astype(F32)
            out_ref[0 if slot == 0 else last] = jnp.where(ok, value, 0.0).astype(BF)


def upsample(count, rows, first, base, recvs, edges, w_up, b_up, skip, outer):
    channels = b_up.shape[0]
    y_len, x_len = skip.shape[1:3]
    total, width = base.shape
    return pl.pallas_call(
        functools.partial(up_kernel, count, rows, outer, len(recvs), first),
        in_specs=[in_vmem() for _ in range(4 + len(recvs) + len(edges))],
        out_specs=in_vmem(),
        out_shape=jax.ShapeDtypeStruct((y_len + 2, x_len, channels), BF),
        scratch_shapes=[
            pltpu.VMEM((total, width), BF),
            pltpu.VMEM((2, channels // 128, 2 * total, 128), F32),
        ],
        compiler_params=pltpu.CompilerParams(vmem_limit_bytes=VMEM_LIMIT),
        cost_estimate=pl.CostEstimate(
            flops=8 * total * width * channels,
            bytes_accessed=2 * total * width,
            transcendentals=0,
        ),
        name="up_outer" if outer else "up_inner",
    )(base, *recvs, *edges, w_up, b_up, skip)


def conv_kernel(layout, chip_of, *refs):
    planes = refs[:4]
    pieces = refs[4 : 4 + len(layout)]
    bias_ref, out_ref, x_ref, w_ref, acc_ref, sem = refs[4 + len(layout) :]
    slab = lax.axis_index("slab")
    core = lax.rem(slab, 2)
    taps, band = pieces[0].shape[:2]
    half = len(pieces) // 2
    copies = []
    for n, plane in enumerate(planes):
        at = jnp.where(core == 0, n, 3 - n)
        copies.append(pltpu.make_async_copy(plane, x_ref.at[at], sem.at[n]))
    groups = ([], [])
    for piece, (step, part) in zip(pieces, layout):
        group = groups[part(0)]
        at = pl.multiple_of(chip_of(slab, step) * band, math.gcd(band, 16))
        dst = w_ref.at[pl.ds(part(core) * taps, taps), pl.ds(at, band), :]
        group.append(pltpu.make_async_copy(piece, dst, sem.at[4 + part(core) * half + len(group)]))
    for copy in copies:
        copy.start()
    for first in range(2):

        @pl.when(core == first)
        def _(first=first):
            for copy in [*groups[first], *groups[1 - first]]:
                copy.start()

    def wait_weights(part):
        for n in range(half):
            pltpu.make_async_copy(
                pieces[0], w_ref.at[pl.ds(part * taps, taps), pl.ds(0, band), :], sem.at[4 + part * half + n]
            ).wait()

    for copy in copies:
        copy.wait()

    y_len, x_len, channels = out_ref.shape[1:]
    size = y_len * x_len
    at_x = lax.rem(lax.broadcasted_iota(jnp.int32, (size, 1), 0), x_len)
    windows = [(dz, dy) for dz in range(3) for dy in range(3)]

    def weight(tap):
        return w_ref[tap if tap < taps else tap + 2 * taps - 27]

    for part, group in enumerate((windows[:4], windows[4:])):
        wait_weights(part)
        rhs = jnp.concatenate(
            [
                jnp.concatenate([weight(9 * dz + 3 * dy + dx) for dx in range(3)], axis=1)
                for dz, dy in group
            ],
            axis=0,
        )
        for j in range(2):
            lhs = jnp.concatenate(
                [x_ref[j + dz, dy : dy + y_len].reshape(size, channels) for dz, dy in group], axis=1
            )
            sums = jnp.dot(lhs, rhs, preferred_element_type=F32)
            if part == 0:
                acc_ref[j] = sums
                continue
            sums = sums + acc_ref[j]
            left, mid, right = (sums[:, i * channels : (i + 1) * channels] for i in range(3))
            left = jnp.where(at_x == 0, 0.0, pltpu.roll(left, 1, 0))
            right = jnp.where(at_x == x_len - 1, 0.0, pltpu.roll(right, size - 1, 0))
            total = left + mid + right + bias_ref[...][None, :]
            total = jnp.where(total > 0, total, 0.01 * total)
            out_ref[j] = total.astype(BF).reshape(y_len, x_len, channels)


def convolve(planes, pieces, layout, chip_of, b_conv, y_len):
    taps, band, channels = pieces[0].shape
    x_len = planes[0].shape[1]
    return pl.pallas_call(
        functools.partial(conv_kernel, layout, chip_of),
        in_specs=[pl.BlockSpec(memory_space=pl.ANY) for _ in [*planes, *pieces]] + [in_vmem()],
        out_specs=in_vmem(),
        out_shape=jax.ShapeDtypeStruct((2, y_len, x_len, channels), BF),
        scratch_shapes=[
            pltpu.VMEM((4, y_len + 2, x_len, channels), BF),
            pltpu.VMEM((2 * taps, channels, channels), BF),
            pltpu.VMEM((2, y_len * x_len, 3 * channels), F32),
            pltpu.SemaphoreType.DMA((4 + len(pieces),)),
        ],
        compiler_params=pltpu.CompilerParams(vmem_limit_bytes=VMEM_LIMIT),
        cost_estimate=pl.CostEstimate(
            flops=2 * 2 * y_len * x_len * 27 * channels * channels,
            bytes_accessed=27 * channels * channels * 2,
            transcendentals=0,
        ),
        name="conv",
    )(*planes, *pieces, b_conv)


def gather_kernel_pieces(w_conv, slabs, core):
    chips = slabs // 2
    taps = (w_conv.shape[0] + 1) // 2
    first_core = core == 0
    low_first = (lambda c: c), (lambda c: 1 - c)
    if (2 * w_conv.shape[1]) % 16:
        whole = lax.all_gather(w_conv, "slab", axis=1, tiled=True)
        pieces = [whole[:taps], whole[w_conv.shape[0] - taps :]]
        return pieces, [(0, lambda c: 0), (0, lambda c: 1)], lambda slab, step: 0
    order = list(range(0, chips, 2)) + list(range(chips - 1, 0, -2))
    mates = [(s, s ^ 1) for s in range(slabs)]
    ring = []
    for at in range(chips):
        ring.append((2 * order[at], 2 * order[(at + 1) % chips]))
        ring.append((2 * order[at] + 1, 2 * order[(at - 1) % chips] + 1))

    def chip_of(slab, step):
        chip, sign = slab // 2, 1 - 2 * lax.rem(slab, 2)
        here = jnp.where(lax.rem(chip, 2) == 0, chip // 2, chips - 1 - chip // 2)
        at = lax.rem(here - sign * step + 2 * chips, chips)
        return jnp.where(2 * at < chips, 2 * at, 2 * (chips - 1 - at) + 1)

    mate = lax.ppermute(w_conv, "slab", mates)
    unit = jnp.concatenate(
        [jnp.where(first_core, w_conv, mate), jnp.where(first_core, mate, w_conv)], axis=1
    )
    low, high = unit[:taps], unit[w_conv.shape[0] - taps :]
    a = jnp.where(first_core, low, high)
    b = jnp.where(first_core, high, low)
    pieces, layout = [a, b], [(0, low_first[0]), (0, low_first[1])]
    for k in range(1, chips // 2 + 1):
        a = lax.ppermute(a, "slab", ring)
        pieces += [a, lax.ppermute(a, "slab", mates)]
        layout += [(k, low_first[0]), (-k, low_first[1])]
        if 2 * k < chips:
            b = lax.ppermute(b, "slab", ring)
            pieces += [b, lax.ppermute(b, "slab", mates)]
            layout += [(k, low_first[1]), (-k, low_first[0])]
    return pieces, layout, chip_of


def on_device(
    tokens,
    mask_index,
    mask_token,
    norm_gain,
    w_in,
    b_in,
    w_out,
    b_out,
    w_up,
    b_up,
    skip,
    w_conv,
    b_conv,
):
    count = lax.axis_size("tp")
    slabs = lax.axis_size("slab")
    me = lax.axis_index("tp")
    slab = lax.axis_index("slab")
    core = slab % 2
    rows, width = tokens.shape
    y_len, x_len, channels = skip.shape[1:]

    def from_peer(k):
        return [((i + k) % count, i) for i in range(count)]

    if count == 2:
        edge = lax.dynamic_index_in_dim(skip, jnp.where(me == 0, y_len - 1, 0), axis=1, keepdims=False)
        packed = jnp.concatenate([tokens, jnp.concatenate([edge[0], edge[1]], axis=1)], axis=0)
        packed = lax.ppermute(packed, "tp", from_peer(1))
        peers = [packed]
        edges, first = [packed], rows
    else:
        peers = [lax.ppermute(tokens, "tp", from_peer(k)) for k in range(1, count)]
        low, high = (jnp.concatenate([skip[0, y], skip[1, y]], axis=1) for y in (y_len - 1, 0))
        edges = [
            lax.ppermute(low, "tp", [(i, i + 1) for i in range(count - 1)]),
            lax.ppermute(high, "tp", [(i + 1, i) for i in range(count - 1)]),
        ]
        first = 0

    pieces, layout, chip_of = gather_kernel_pieces(w_conv, slabs, core)

    base, *sends = mlp(tokens, peers, mask_index, mask_token, norm_gain, w_in, b_in, w_out, b_out)
    recvs = [
        lax.ppermute(s, "tp", [(i, (i + k) % count) for i in range(count)])
        for k, s in enumerate(sends, start=1)
    ]

    up = functools.partial(upsample, count, rows, first, base, recvs, edges, w_up, b_up, skip)
    pairs = [(s, s + 1) for s in range(1, slabs - 1, 2)]
    outer = up(True)
    beyond = lax.ppermute(outer, "slab", pairs + [(t, s) for s, t in pairs])
    inner = up(False)
    mates = lax.ppermute(inner, "slab", [(s, s ^ 1) for s in range(slabs)])

    return convolve([beyond, outer, inner, mates], pieces, layout, chip_of, b_conv, y_len)


def solution(mesh):
    in_specs = (
        P(("slab", "tp"), None),
        P(),
        P(),
        P(),
        P(None, "tp"),
        P("tp"),
        P("tp", None),
        P(),
        P(),
        P(),
        P("slab", "tp", None, None),
        P(None, "slab", None),
        P(),
    )
    out_specs = P("slab", "tp", None, None)
    return jax.shard_map(
        on_device, mesh=mesh, in_specs=in_specs, out_specs=out_specs, check_vma=False
    )
```

```python
import functools
import math

import jax
import jax.numpy as jnp
from jax import lax
from jax.experimental import pallas as pl
from jax.experimental.pallas import tpu as pltpu
from jax.sharding import PartitionSpec as P

BF = jnp.bfloat16
F32 = jnp.float32
BX = 32
MIB = 1024 * 1024


def in_vmem(*_):
    return pl.BlockSpec(memory_space=pltpu.VMEM)


def in_smem(*_):
    return pl.BlockSpec(memory_space=pltpu.SMEM)


def mlp_kernel(count, rows, chunk, mask_ref, mtok_ref, gain_ref, bout_ref, bin_ref, *refs):
    toks = refs[:count]
    w_in_ref, w_out_ref = refs[count : count + 2]
    base_ref = refs[count + 2]
    sends = refs[count + 3 : 2 * count + 2]
    normed_ref, filled_ref, acc_ref = refs[2 * count + 2 :]
    me = lax.axis_index("tp")
    plane = lax.axis_index("slab") * (count * rows)

    index = mask_ref[...][None, :]
    mask_token = mtok_ref[...].astype(F32)[None, :]
    gain = gain_ref[...][None, :]
    for k in range(count):
        first = plane + lax.rem(me + k, count) * rows
        ids = lax.broadcasted_iota(jnp.int32, (rows, 1), 0) + first
        hit = jnp.where(index == ids, 1.0, 0.0)
        flag = jnp.max(hit, axis=1, keepdims=True)
        values = jnp.where(flag > 0.5, mask_token, toks[k][0:rows, :].astype(F32))
        mean = jnp.mean(values, axis=1, keepdims=True)
        cent = values - mean
        var = jnp.mean(cent * cent, axis=1, keepdims=True)
        normed = cent * lax.rsqrt(var + 1e-05) * gain
        normed_ref[k * rows : (k + 1) * rows, :] = normed.astype(BF)
        filled_ref[k * rows : (k + 1) * rows, :] = values

    hidden_size = w_in_ref.shape[1]
    for at in range(0, hidden_size, chunk):
        pre = jnp.dot(normed_ref[...], w_in_ref[:, at : at + chunk], preferred_element_type=F32)
        pre = pre + bin_ref[at : at + chunk][None, :]
        hidden = (0.5 * pre * (1.0 + lax.erf(pre * math.sqrt(0.5)))).astype(BF)
        part = jnp.dot(hidden, w_out_ref[at : at + chunk, :], preferred_element_type=F32)
        if at == 0:
            acc_ref[...] = part
        else:
            acc_ref[...] += part

    bout = bout_ref[...][None, :]
    for k in range(count):
        parts = [(pl.ds(k * rows, rows), 0, rows)]
        if count == 2:
            low = lax.rem(me + k, count) == 0
            start = ((k + 1) % 2) * rows + jnp.where(low, 0, rows - BX)
            parts.append((pl.ds(pl.multiple_of(start, BX), BX), rows, BX))
        else:
            parts.append((pl.ds(((k - 1) % count) * rows + rows - BX, BX), rows, BX))
            parts.append((pl.ds(((k + 1) % count) * rows, BX), rows + BX, BX))
        for src, dst, size in parts:
            if k == 0:
                base_ref[dst : dst + size, :] = acc_ref[src, :] + filled_ref[src, :] + bout
            else:
                sends[k - 1][dst : dst + size, :] = acc_ref[src, :].astype(BF)


def mlp(tokens, peers, mask_index, mask_token, norm_gain, w_in, b_in, w_out, b_out):
    count = len(peers) + 1
    rows, width = tokens.shape
    hidden = w_in.shape[1]
    chunk = next(c for c in (256, 128, hidden) if hidden % c == 0)
    total = rows + (1 if count == 2 else 2) * BX
    outs = [jax.ShapeDtypeStruct((total, width), F32)] + [
        jax.ShapeDtypeStruct((total, width), BF) for _ in peers
    ]
    return pl.pallas_call(
        functools.partial(mlp_kernel, count, rows, chunk),
        in_specs=[in_vmem() for _ in range(8 + len(peers))],
        out_specs=[in_vmem() for _ in outs],
        out_shape=outs,
        scratch_shapes=[
            pltpu.VMEM((count * rows, width), BF),
            pltpu.VMEM((count * rows, width), F32),
            pltpu.VMEM((count * rows, width), F32),
        ],
        compiler_params=pltpu.CompilerParams(vmem_limit_bytes=16 * MIB),
        cost_estimate=pl.CostEstimate(
            flops=4 * count * rows * width * hidden,
            bytes_accessed=4 * width * hidden,
            transcendentals=count * rows * hidden,
        ),
        name="mlp",
    )(mask_index, mask_token, norm_gain, b_out, b_in, tokens, *peers, w_in, w_out)


def up_kernel(count, rows, outer, arrived, first, base_ref, *refs):
    recvs = refs[:arrived]
    edges = refs[arrived : arrived + (1 if count == 2 else 2)]
    w_ref, bup_ref, skip_ref, out_ref, bott_ref, wide_ref = refs[arrived + len(edges) :]
    core = lax.rem(lax.axis_index("slab"), 2)
    me = lax.axis_index("tp")
    a = core if outer else 1 - core
    channels = bup_ref.shape[0]
    y_rows = rows // BX
    last = out_ref.shape[0] - 1
    bias = bup_ref[...][None, :]

    total = base_ref[...]
    for r in recvs:
        total = total + r[...].astype(F32)
    bott_ref[...] = total.astype(BF)
    size = total.shape[0]
    mine = pl.ds(pl.multiple_of(a * channels, 128), channels)

    for b in range(2):
        start = pl.multiple_of((4 * a + 2 * b) * channels, 128)
        up = jnp.dot(bott_ref[...], w_ref[:, pl.ds(start, 2 * channels)], preferred_element_type=F32)
        for c in range(2):
            for l in range(0, channels, 128):
                wide_ref[b, l // 128, pl.ds(c, size, stride=2), :] = up[
                    :, c * channels + l : c * channels + l + 128
                ]

        def fine_row(at):
            return jnp.concatenate(
                [
                    wide_ref[b, l // 128, at * 2 * BX : (at + 1) * 2 * BX, :]
                    for l in range(0, channels, 128)
                ],
                axis=1,
            )

        for y in range(y_rows):
            row = fine_row(y) + bias + skip_ref[a, 2 * y + b].astype(F32)
            out_ref[1 + 2 * y + b] = row.astype(BF)
        if count == 2:
            value = fine_row(y_rows) + bias + edges[0][first:, mine].astype(F32)
            used = me == b
            out_ref[last if b == 0 else 0] = jnp.where(used, value, 0.0).astype(BF)
        else:
            slot = 1 - b
            ok = (me > 0) if slot == 0 else (me < count - 1)
            value = fine_row(y_rows + slot) + bias + edges[slot][first:, mine].astype(F32)
            out_ref[0 if slot == 0 else last] = jnp.where(ok, value, 0.0).astype(BF)


def upsample(count, rows, first, base, recvs, edges, w_up, b_up, skip, outer):
    channels = b_up.shape[0]
    y_len, x_len = skip.shape[1:3]
    total, width = base.shape
    return pl.pallas_call(
        functools.partial(up_kernel, count, rows, outer, len(recvs), first),
        in_specs=[in_vmem() for _ in range(4 + len(recvs) + len(edges))],
        out_specs=in_vmem(),
        out_shape=jax.ShapeDtypeStruct((y_len + 2, x_len, channels), BF),
        scratch_shapes=[
            pltpu.VMEM((total, width), BF),
            pltpu.VMEM((2, channels // 128, 2 * total, 128), F32),
        ],
        compiler_params=pltpu.CompilerParams(vmem_limit_bytes=16 * MIB),
        cost_estimate=pl.CostEstimate(
            flops=8 * total * width * channels,
            bytes_accessed=2 * total * width,
            transcendentals=0,
        ),
        name="up_outer" if outer else "up_inner",
    )(base, *recvs, *edges, w_up, b_up, skip)


def conv_kernel(layout, chip_of, *refs):
    planes = refs[:4]
    pieces = refs[4 : 4 + len(layout)]
    bias_ref, out_ref, x_ref, w_ref, acc_ref, sem = refs[4 + len(layout) :]
    slab = lax.axis_index("slab")
    core = lax.rem(slab, 2)
    taps, band = pieces[0].shape[:2]
    half = len(pieces) // 2
    copies = []
    for n, plane in enumerate(planes):
        at = jnp.where(core == 0, n, 3 - n)
        copies.append(pltpu.make_async_copy(plane, x_ref.at[at], sem.at[n]))
    groups = ([], [])
    for piece, (step, part) in zip(pieces, layout):
        group = groups[part(0)]
        at = pl.multiple_of(chip_of(slab, step) * band, math.gcd(band, 16))
        dst = w_ref.at[pl.ds(part(core) * taps, taps), pl.ds(at, band), :]
        group.append(pltpu.make_async_copy(piece, dst, sem.at[4 + part(core) * half + len(group)]))
    for copy in copies:
        copy.start()
    for first in range(2):

        @pl.when(core == first)
        def _(first=first):
            for copy in [*groups[first], *groups[1 - first]]:
                copy.start()

    def wait_weights(part):
        for n in range(half):
            pltpu.make_async_copy(
                pieces[0], w_ref.at[pl.ds(part * taps, taps), pl.ds(0, band), :], sem.at[4 + part * half + n]
            ).wait()

    for copy in copies:
        copy.wait()

    y_len, x_len, channels = out_ref.shape[1:]
    size = y_len * x_len
    at_x = lax.rem(lax.broadcasted_iota(jnp.int32, (size, 1), 0), x_len)
    windows = [(dz, dy) for dz in range(3) for dy in range(3)]

    def weight(tap):
        return w_ref[tap if tap < taps else tap + 2 * taps - 27]

    for part, group in enumerate((windows[:4], windows[4:])):
        wait_weights(part)
        rhs = jnp.concatenate(
            [
                jnp.concatenate([weight(9 * dz + 3 * dy + dx) for dx in range(3)], axis=1)
                for dz, dy in group
            ],
            axis=0,
        )
        for j in range(2):
            lhs = jnp.concatenate(
                [x_ref[j + dz, dy : dy + y_len].reshape(size, channels) for dz, dy in group], axis=1
            )
            sums = jnp.dot(lhs, rhs, preferred_element_type=F32)
            if part == 0:
                acc_ref[j] = sums
                continue
            sums = sums + acc_ref[j]
            left, mid, right = (sums[:, i * channels : (i + 1) * channels] for i in range(3))
            left = jnp.where(at_x == 0, 0.0, pltpu.roll(left, 1, 0))
            right = jnp.where(at_x == x_len - 1, 0.0, pltpu.roll(right, size - 1, 0))
            total = left + mid + right + bias_ref[...][None, :]
            total = jnp.where(total > 0, total, 0.01 * total)
            out_ref[j] = total.astype(BF).reshape(y_len, x_len, channels)


def convolve(planes, pieces, layout, chip_of, b_conv, y_len):
    taps, band, channels = pieces[0].shape
    x_len = planes[0].shape[1]
    return pl.pallas_call(
        functools.partial(conv_kernel, layout, chip_of),
        in_specs=[pl.BlockSpec(memory_space=pl.ANY) for _ in [*planes, *pieces]] + [in_vmem()],
        out_specs=in_vmem(),
        out_shape=jax.ShapeDtypeStruct((2, y_len, x_len, channels), BF),
        scratch_shapes=[
            pltpu.VMEM((4, y_len + 2, x_len, channels), BF),
            pltpu.VMEM((2 * taps, channels, channels), BF),
            pltpu.VMEM((2, y_len * x_len, 3 * channels), F32),
            pltpu.SemaphoreType.DMA((4 + len(pieces),)),
        ],
        compiler_params=pltpu.CompilerParams(vmem_limit_bytes=28 * MIB),
        cost_estimate=pl.CostEstimate(
            flops=2 * 2 * y_len * x_len * 27 * channels * channels,
            bytes_accessed=27 * channels * channels * 2,
            transcendentals=0,
        ),
        name="conv",
    )(*planes, *pieces, b_conv)


def gather_kernel_pieces(w_conv, slabs, core):
    chips = slabs // 2
    taps = (w_conv.shape[0] + 1) // 2
    first_core = core == 0
    low_first = (lambda c: c), (lambda c: 1 - c)
    if (2 * w_conv.shape[1]) % 16:
        whole = lax.all_gather(w_conv, "slab", axis=1, tiled=True)
        pieces = [whole[:taps], whole[w_conv.shape[0] - taps :]]
        return pieces, [(0, lambda c: 0), (0, lambda c: 1)], lambda slab, step: 0
    order = list(range(0, chips, 2)) + list(range(chips - 1, 0, -2))
    mates = [(s, s ^ 1) for s in range(slabs)]
    ring = []
    for at in range(chips):
        ring.append((2 * order[at], 2 * order[(at + 1) % chips]))
        ring.append((2 * order[at] + 1, 2 * order[(at - 1) % chips] + 1))

    def chip_of(slab, step):
        chip, sign = slab // 2, 1 - 2 * lax.rem(slab, 2)
        here = jnp.where(lax.rem(chip, 2) == 0, chip // 2, chips - 1 - chip // 2)
        at = lax.rem(here - sign * step + 2 * chips, chips)
        return jnp.where(2 * at < chips, 2 * at, 2 * (chips - 1 - at) + 1)

    mate = lax.ppermute(w_conv, "slab", mates)
    unit = jnp.concatenate(
        [jnp.where(first_core, w_conv, mate), jnp.where(first_core, mate, w_conv)], axis=1
    )
    low, high = unit[:taps], unit[w_conv.shape[0] - taps :]
    a = jnp.where(first_core, low, high)
    b = jnp.where(first_core, high, low)
    pieces, layout = [a, b], [(0, low_first[0]), (0, low_first[1])]
    for k in range(1, chips // 2 + 1):
        a = lax.ppermute(a, "slab", ring)
        pieces += [a, lax.ppermute(a, "slab", mates)]
        layout += [(k, low_first[0]), (-k, low_first[1])]
        if 2 * k < chips:
            b = lax.ppermute(b, "slab", ring)
            pieces += [b, lax.ppermute(b, "slab", mates)]
            layout += [(k, low_first[1]), (-k, low_first[0])]
    return pieces, layout, chip_of


def on_device(
    tokens,
    mask_index,
    mask_token,
    norm_gain,
    w_in,
    b_in,
    w_out,
    b_out,
    w_up,
    b_up,
    skip,
    w_conv,
    b_conv,
):
    count = lax.axis_size("tp")
    slabs = lax.axis_size("slab")
    me = lax.axis_index("tp")
    slab = lax.axis_index("slab")
    core = slab % 2
    rows, width = tokens.shape
    y_len, x_len, channels = skip.shape[1:]

    def from_peer(k):
        return [((i + k) % count, i) for i in range(count)]

    if count == 2:
        edge = lax.dynamic_index_in_dim(skip, jnp.where(me == 0, y_len - 1, 0), axis=1, keepdims=False)
        packed = jnp.concatenate([tokens, jnp.concatenate([edge[0], edge[1]], axis=1)], axis=0)
        packed = lax.ppermute(packed, "tp", from_peer(1))
        peers = [packed]
        edges, first = [packed], rows
    else:
        peers = [lax.ppermute(tokens, "tp", from_peer(k)) for k in range(1, count)]
        low, high = (jnp.concatenate([skip[0, y], skip[1, y]], axis=1) for y in (y_len - 1, 0))
        edges = [
            lax.ppermute(low, "tp", [(i, i + 1) for i in range(count - 1)]),
            lax.ppermute(high, "tp", [(i + 1, i) for i in range(count - 1)]),
        ]
        first = 0

    pieces, layout, chip_of = gather_kernel_pieces(w_conv, slabs, core)

    base, *sends = mlp(tokens, peers, mask_index, mask_token, norm_gain, w_in, b_in, w_out, b_out)
    recvs = [
        lax.ppermute(s, "tp", [(i, (i + k) % count) for i in range(count)])
        for k, s in enumerate(sends, start=1)
    ]

    up = functools.partial(upsample, count, rows, first, base, recvs, edges, w_up, b_up, skip)
    pairs = [(s, s + 1) for s in range(1, slabs - 1, 2)]
    outer = up(True)
    beyond = lax.ppermute(outer, "slab", pairs + [(t, s) for s, t in pairs])
    inner = up(False)
    mates = lax.ppermute(inner, "slab", [(s, s ^ 1) for s in range(slabs)])

    return convolve([beyond, outer, inner, mates], pieces, layout, chip_of, b_conv, y_len)


def solution(mesh):
    in_specs = (
        P(("slab", "tp"), None),
        P(),
        P(),
        P(),
        P(None, "tp"),
        P("tp"),
        P("tp", None),
        P(),
        P(),
        P(),
        P("slab", "tp", None, None),
        P(None, "slab", None),
        P(),
    )
    out_specs = P("slab", "tp", None, None)
    return jax.shard_map(
        on_device, mesh=mesh, in_specs=in_specs, out_specs=out_specs, check_vma=False
    )
```

```python
import functools
import math

import jax
import jax.numpy as jnp
from jax import lax
from jax.experimental import pallas as pl
from jax.experimental.pallas import tpu as pltpu
from jax.sharding import PartitionSpec as P

BF = jnp.bfloat16
F32 = jnp.float32
BX = 32
MIB = 1024 * 1024
FLAG_FLOPS = 6 * 10**9
HELP = False


def in_vmem(*_):
    return pl.BlockSpec(memory_space=pltpu.VMEM)


def in_smem(*_):
    return pl.BlockSpec(memory_space=pltpu.SMEM)


def mask_kernel(count, rows, mask_ref, flag_ref):
    me = lax.axis_index("tp")
    plane = lax.axis_index("slab") * (count * rows)
    index = mask_ref[...][None, :]
    for k in range(count):
        first = plane + lax.rem(me + k, count) * rows
        ids = lax.broadcasted_iota(jnp.int32, (rows, 1), 0) + first
        hit = jnp.max(jnp.where(index == ids, 1.0, 0.0), axis=1, keepdims=True)
        flag_ref[k * rows : (k + 1) * rows, :] = jnp.broadcast_to(hit, (rows, flag_ref.shape[1]))


def mask_of(count, rows, mask_index):
    return pl.pallas_call(
        functools.partial(mask_kernel, count, rows),
        in_specs=[in_vmem()],
        out_specs=in_vmem(),
        out_shape=jax.ShapeDtypeStruct((count * rows, 128), F32),
        compiler_params=pltpu.CompilerParams(vmem_limit_bytes=4 * MIB),
        cost_estimate=pl.CostEstimate(flops=FLAG_FLOPS, bytes_accessed=4 * MIB, transcendentals=0),
        name="mask",
    )(mask_index)


def mlp_kernel(count, rows, chunk, flag_ref, mtok_ref, gain_ref, bout_ref, bin_ref, *refs):
    toks = refs[:count]
    w_in_ref, w_out_ref = refs[count : count + 2]
    base_ref = refs[count + 2]
    sends = refs[count + 3 : 2 * count + 2]
    normed_ref, filled_ref, acc_ref = refs[2 * count + 2 :]
    me = lax.axis_index("tp")
    mask_token = mtok_ref[...].astype(F32)[None, :]
    gain = gain_ref[...][None, :]
    for k in range(count):
        flag = flag_ref[k * rows : (k + 1) * rows, 0:1]
        values = jnp.where(flag > 0.5, mask_token, toks[k][0:rows, :].astype(F32))
        mean = jnp.mean(values, axis=1, keepdims=True)
        cent = values - mean
        var = jnp.mean(cent * cent, axis=1, keepdims=True)
        normed = cent * lax.rsqrt(var + 1e-05) * gain
        normed_ref[k * rows : (k + 1) * rows, :] = normed.astype(BF)
        filled_ref[k * rows : (k + 1) * rows, :] = values

    hidden_size = w_in_ref.shape[1]
    for at in range(0, hidden_size, chunk):
        pre = jnp.dot(normed_ref[...], w_in_ref[:, at : at + chunk], preferred_element_type=F32)
        pre = pre + bin_ref[at : at + chunk][None, :]
        hidden = (0.5 * pre * (1.0 + lax.erf(pre * math.sqrt(0.5)))).astype(BF)
        part = jnp.dot(hidden, w_out_ref[at : at + chunk, :], preferred_element_type=F32)
        if at == 0:
            acc_ref[...] = part
        else:
            acc_ref[...] += part

    bout = bout_ref[...][None, :]
    for k in range(count):
        parts = [(pl.ds(k * rows, rows), 0, rows)]
        if count == 2:
            low = lax.rem(me + k, count) == 0
            start = ((k + 1) % 2) * rows + jnp.where(low, 0, rows - BX)
            parts.append((pl.ds(pl.multiple_of(start, BX), BX), rows, BX))
        else:
            parts.append((pl.ds(((k - 1) % count) * rows + rows - BX, BX), rows, BX))
            parts.append((pl.ds(((k + 1) % count) * rows, BX), rows + BX, BX))
        for src, dst, size in parts:
            if k == 0:
                base_ref[dst : dst + size, :] = acc_ref[src, :] + filled_ref[src, :] + bout
            else:
                sends[k - 1][dst : dst + size, :] = acc_ref[src, :].astype(BF)


def mlp(tokens, peers, flags, mask_token, norm_gain, w_in, b_in, w_out, b_out):
    count = len(peers) + 1
    rows, width = tokens.shape
    hidden = w_in.shape[1]
    chunk = next(c for c in (256, 128, hidden) if hidden % c == 0)
    total = rows + (1 if count == 2 else 2) * BX
    outs = [jax.ShapeDtypeStruct((total, width), F32)] + [
        jax.ShapeDtypeStruct((total, width), BF) for _ in peers
    ]
    return pl.pallas_call(
        functools.partial(mlp_kernel, count, rows, chunk),
        in_specs=[in_vmem() for _ in range(8 + len(peers))],
        out_specs=[in_vmem() for _ in outs],
        out_shape=outs,
        scratch_shapes=[
            pltpu.VMEM((count * rows, width), BF),
            pltpu.VMEM((count * rows, width), F32),
            pltpu.VMEM((count * rows, width), F32),
        ],
        compiler_params=pltpu.CompilerParams(vmem_limit_bytes=16 * MIB),
        cost_estimate=pl.CostEstimate(
            flops=4 * count * rows * width * hidden,
            bytes_accessed=4 * width * hidden,
            transcendentals=count * rows * hidden,
        ),
        name="mlp",
    )(flags, mask_token, norm_gain, b_out, b_in, tokens, *peers, w_in, w_out)


def up_kernel(count, rows, arrived, first, base_ref, *refs):
    recvs = refs[:arrived]
    edges = refs[arrived : arrived + (1 if count == 2 else 2)]
    w_ref, bup_ref, skip_ref, outer_ref, inner_ref, bott_ref, wide_ref = refs[arrived + len(edges) :]
    core = lax.rem(lax.axis_index("slab"), 2)
    me = lax.axis_index("tp")
    channels = bup_ref.shape[0]
    y_rows = rows // BX
    last = outer_ref.shape[0] - 1
    bias = bup_ref[...][None, :]

    total = base_ref[...]
    for r in recvs:
        total = total + r[...].astype(F32)
    bott_ref[...] = total.astype(BF)
    size = total.shape[0]

    for out_ref, b in [(ref, b) for ref in (outer_ref, inner_ref) for b in range(2)]:
        a = core if out_ref is outer_ref else 1 - core
        mine = pl.ds(pl.multiple_of(a * channels, 128), channels)
        start = pl.multiple_of((4 * a + 2 * b) * channels, 128)
        up = jnp.dot(bott_ref[...], w_ref[:, pl.ds(start, 2 * channels)], preferred_element_type=F32)
        for c in range(2):
            for l in range(0, channels, 128):
                wide_ref[b, l // 128, pl.ds(c, size, stride=2), :] = up[
                    :, c * channels + l : c * channels + l + 128
                ]

        def fine_row(at, b=b):
            return jnp.concatenate(
                [
                    wide_ref[b, l // 128, at * 2 * BX : (at + 1) * 2 * BX, :]
                    for l in range(0, channels, 128)
                ],
                axis=1,
            )

        for y in range(y_rows):
            row = fine_row(y) + bias + skip_ref[a, 2 * y + b].astype(F32)
            out_ref[1 + 2 * y + b] = row.astype(BF)
        if count == 2:
            value = fine_row(y_rows) + bias + edges[0][first:, mine].astype(F32)
            used = me == b
            out_ref[last if b == 0 else 0] = jnp.where(used, value, 0.0).astype(BF)
        else:
            slot = 1 - b
            ok = (me > 0) if slot == 0 else (me < count - 1)
            value = fine_row(y_rows + slot) + bias + edges[slot][first:, mine].astype(F32)
            out_ref[0 if slot == 0 else last] = jnp.where(ok, value, 0.0).astype(BF)


def upsample(count, rows, first, base, recvs, edges, w_up, b_up, skip):
    channels = b_up.shape[0]
    y_len, x_len = skip.shape[1:3]
    total, width = base.shape
    return pl.pallas_call(
        functools.partial(up_kernel, count, rows, len(recvs), first),
        in_specs=[in_vmem() for _ in range(4 + len(recvs) + len(edges))],
        out_specs=[in_vmem()] * 2,
        out_shape=[jax.ShapeDtypeStruct((y_len + 2, x_len, channels), BF)] * 2,
        scratch_shapes=[
            pltpu.VMEM((total, width), BF),
            pltpu.VMEM((2, channels // 128, 2 * total, 128), F32),
        ],
        compiler_params=pltpu.CompilerParams(vmem_limit_bytes=16 * MIB),
        cost_estimate=pl.CostEstimate(
            flops=16 * total * width * channels,
            bytes_accessed=2 * total * width,
            transcendentals=0,
        ),
        name="upsample",
    )(base, *recvs, *edges, w_up, b_up, skip)


def conv_kernel(units, chip_of, *refs):
    planes = refs[:4]
    count = len(jax.tree.leaves([unit[1:] for unit in units]))
    pieces = [(step, *jax.tree.map(lambda n: refs[4 + n], rest)) for step, *rest in units]
    bias_ref, out_ref, x_ref, w_ref, acc_ref, sem = refs[4 + count :]
    slab, me = lax.axis_index("slab"), lax.axis_index("tp")
    core = lax.rem(slab, 2)
    copies = []
    for n, plane in enumerate(planes):
        at = jnp.where(core == 0, n, 3 - n)
        copies.append(pltpu.make_async_copy(plane, x_ref.at[at], sem.at[n]))
    for copy in copies:
        copy.start()

    def rows_of(piece, tap):
        if not isinstance(piece, tuple):
            return piece[tap]
        kept, other = piece
        taps = kept.shape[0]
        if tap < taps:
            return jnp.where(lax.rem(me, 2) == 0, kept[tap], other[tap])
        return jnp.where(lax.rem(me, 2) == 0, other[tap - (27 - taps)], kept[tap - (27 - taps)])

    def assemble(taps):
        for step, mine, theirs in pieces:
            for tap in taps:
                a, b = rows_of(mine, tap), rows_of(theirs, tap)
                band = a.shape[0] + b.shape[0]
                at = pl.multiple_of(chip_of(slab, step) * band, 16)
                w_ref[tap, pl.ds(at, band), :] = jnp.concatenate(
                    [jnp.where(core == 0, a, b), jnp.where(core == 0, b, a)], axis=0
                )

    y_len, x_len, channels = out_ref.shape[1:]
    size = y_len * x_len
    at_x = lax.rem(lax.broadcasted_iota(jnp.int32, (size, 1), 0), x_len)
    windows = [(dz, dy) for dz in range(3) for dy in range(3)]

    for part, group in enumerate((windows[:4], windows[4:])):
        taps = [9 * dz + 3 * dy + dx for dz, dy in group for dx in range(3)]
        if len(pieces) > 1:
            assemble(taps)
        weights = w_ref if len(pieces) > 1 else pieces[0][1]
        if part == 0:
            for copy in copies:
                copy.wait()
        rhs = jnp.concatenate(
            [
                jnp.concatenate([weights[9 * dz + 3 * dy + dx] for dx in range(3)], axis=1)
                for dz, dy in group
            ],
            axis=0,
        )
        for j in range(2):
            lhs = jnp.concatenate(
                [x_ref[j + dz, dy : dy + y_len].reshape(size, channels) for dz, dy in group], axis=1
            )
            sums = jnp.dot(lhs, rhs, preferred_element_type=F32)
            if part == 0:
                acc_ref[j] = sums
                continue
            sums = sums + acc_ref[j]
            left, mid, right = (sums[:, i * channels : (i + 1) * channels] for i in range(3))
            left = jnp.where(at_x == 0, 0.0, pltpu.roll(left, 1, 0))
            right = jnp.where(at_x == x_len - 1, 0.0, pltpu.roll(right, size - 1, 0))
            total = left + mid + right + bias_ref[...][None, :]
            total = jnp.where(total > 0, total, 0.01 * total)
            out_ref[j] = total.astype(BF).reshape(y_len, x_len, channels)


def convolve(planes, units, chip_of, b_conv, y_len):
    x_len, channels = planes[0].shape[1:]
    pieces = jax.tree.leaves([unit[1:] for unit in units])
    numbered = iter(range(len(pieces)))
    marks = [(step, *jax.tree.map(lambda _: next(numbered), rest)) for step, *rest in units]
    return pl.pallas_call(
        functools.partial(conv_kernel, marks, chip_of),
        in_specs=[pl.BlockSpec(memory_space=pl.ANY) for _ in planes]
        + [in_vmem() for _ in [*pieces, b_conv]],
        out_specs=in_vmem(),
        out_shape=jax.ShapeDtypeStruct((2, y_len, x_len, channels), BF),
        scratch_shapes=[
            pltpu.VMEM((4, y_len + 2, x_len, channels), BF),
            pltpu.VMEM((27, channels, channels), BF),
            pltpu.VMEM((2, y_len * x_len, 3 * channels), F32),
            pltpu.SemaphoreType.DMA((4,)),
        ],
        compiler_params=pltpu.CompilerParams(vmem_limit_bytes=32 * MIB),
        cost_estimate=pl.CostEstimate(
            flops=2 * 2 * y_len * x_len * 27 * channels * channels,
            bytes_accessed=27 * channels * channels * 2,
            transcendentals=0,
        ),
        name="conv",
    )(*planes, *pieces, b_conv)


def gather_weights(w_conv, slabs, count):
    chips = slabs // 2
    if count != 2 or chips % 2 or chips < 6 or (2 * w_conv.shape[1]) % 16:
        whole = lax.all_gather(w_conv, "slab", axis=1, tiled=True)
        return [(0, whole)], None
    order = list(range(0, chips, 2)) + list(range(chips - 1, 0, -2))
    mates = [(s, s ^ 1) for s in range(slabs)]
    pairs = [(i, i ^ 1) for i in range(count)]
    ring = []
    for at in range(chips):
        ring.append((2 * order[at], 2 * order[(at + 1) % chips]))
        ring.append((2 * order[at] + 1, 2 * order[(at - 1) % chips] + 1))

    def chip_of(slab, step):
        chip, sign = slab // 2, 1 - 2 * lax.rem(slab, 2)
        here = jnp.where(lax.rem(chip, 2) == 0, chip // 2, chips - 1 - chip // 2)
        at = lax.rem(here - sign * step + 2 * chips, chips)
        return jnp.where(2 * at < chips, 2 * at, 2 * (chips - 1 - at) + 1)

    pp = lax.ppermute
    last = chips // 2
    a = pp(w_conv, "slab", ring)
    if HELP:
        taps = w_conv.shape[0]
        half = (taps + 1) // 2
        part = lax.dynamic_slice_in_dim(w_conv, lax.axis_index("tp") * (taps - half), half, axis=0)
        units = [(0, w_conv, pp(w_conv, "slab", mates))]
        b = pp(part, "slab", mates)
    else:
        b = pp(w_conv, "slab", mates)
        units = [(0, w_conv, b)]
    for k in range(1, last + 1):
        a_mate = pp(a, "slab", mates)
        if k == last:
            units.append((k, a, a_mate))
            break
        b = pp(b, "slab", ring)
        both = (b, pp(b, "tp", pairs)) if HELP else b
        both_mate = jax.tree.map(lambda h: pp(h, "slab", mates), both)
        units.append((k, a, both))
        units.append((-k, both_mate, a_mate))
        a = pp(a, "slab", ring)
    return units, chip_of


def on_device(
    tokens,
    mask_index,
    mask_token,
    norm_gain,
    w_in,
    b_in,
    w_out,
    b_out,
    w_up,
    b_up,
    skip,
    w_conv,
    b_conv,
):
    count = lax.axis_size("tp")
    slabs = lax.axis_size("slab")
    me = lax.axis_index("tp")
    rows, width = tokens.shape
    y_len, x_len, channels = skip.shape[1:]

    def from_peer(k):
        return [((i + k) % count, i) for i in range(count)]

    if count == 2:
        edge = lax.dynamic_index_in_dim(skip, jnp.where(me == 0, y_len - 1, 0), axis=1, keepdims=False)
        packed = jnp.concatenate([tokens, jnp.concatenate([edge[0], edge[1]], axis=1)], axis=0)
        packed = lax.ppermute(packed, "tp", from_peer(1))
        peers = [packed]
        edges, first = [packed], rows
    else:
        peers = [lax.ppermute(tokens, "tp", from_peer(k)) for k in range(1, count)]
        low, high = (jnp.concatenate([skip[0, y], skip[1, y]], axis=1) for y in (y_len - 1, 0))
        edges = [
            lax.ppermute(low, "tp", [(i, i + 1) for i in range(count - 1)]),
            lax.ppermute(high, "tp", [(i + 1, i) for i in range(count - 1)]),
        ]
        first = 0

    units, chip_of = gather_weights(w_conv, slabs, count)

    base, *sends = mlp(tokens, peers, mask_of(count, rows, mask_index), mask_token, norm_gain, w_in, b_in, w_out, b_out)
    recvs = [
        lax.ppermute(s, "tp", [(i, (i + k) % count) for i in range(count)])
        for k, s in enumerate(sends, start=1)
    ]
    outer, inner = upsample(count, rows, first, base, recvs, edges, w_up, b_up, skip)
    pairs = [(s, s + 1) for s in range(1, slabs - 1, 2)]
    beyond = lax.ppermute(outer, "slab", pairs + [(t, s) for s, t in pairs])
    mates = lax.ppermute(inner, "slab", [(s, s ^ 1) for s in range(slabs)])
    return convolve([beyond, outer, inner, mates], units, chip_of, b_conv, y_len)


def solution(mesh):
    in_specs = (
        P(("slab", "tp"), None),
        P(),
        P(),
        P(),
        P(None, "tp"),
        P("tp"),
        P("tp", None),
        P(),
        P(),
        P(),
        P("slab", "tp", None, None),
        P(None, "slab", None),
        P(),
    )
    out_specs = P("slab", "tp", None, None)
    return jax.shard_map(
        on_device, mesh=mesh, in_specs=in_specs, out_specs=out_specs, check_vma=False
    )
```

```python
import functools
import math

import jax
import jax.numpy as jnp
from jax import lax
from jax.experimental import pallas as pl
from jax.experimental.pallas import tpu as pltpu
from jax.sharding import PartitionSpec as P

BF = jnp.bfloat16
F32 = jnp.float32
BX = 32
MIB = 1024 * 1024
FLAG_FLOPS = 6 * 10**9


def in_vmem(*_):
    return pl.BlockSpec(memory_space=pltpu.VMEM)


def in_smem(*_):
    return pl.BlockSpec(memory_space=pltpu.SMEM)


def mask_kernel(count, rows, mask_ref, flag_ref):
    me = lax.axis_index("tp")
    plane = lax.axis_index("slab") * (count * rows)
    index = mask_ref[...][None, :]
    for k in range(count):
        first = plane + lax.rem(me + k, count) * rows
        ids = lax.broadcasted_iota(jnp.int32, (rows, 1), 0) + first
        hit = jnp.max(jnp.where(index == ids, 1.0, 0.0), axis=1, keepdims=True)
        flag_ref[k * rows : (k + 1) * rows, :] = jnp.broadcast_to(hit, (rows, flag_ref.shape[1]))


def mask_of(count, rows, mask_index):
    return pl.pallas_call(
        functools.partial(mask_kernel, count, rows),
        in_specs=[in_vmem()],
        out_specs=in_vmem(),
        out_shape=jax.ShapeDtypeStruct((count * rows, 128), F32),
        compiler_params=pltpu.CompilerParams(vmem_limit_bytes=4 * MIB),
        cost_estimate=pl.CostEstimate(flops=FLAG_FLOPS, bytes_accessed=4 * MIB, transcendentals=0),
        name="mask",
    )(mask_index)


def mlp_kernel(count, rows, chunk, flag_ref, mtok_ref, gain_ref, bout_ref, bin_ref, *refs):
    toks = refs[:count]
    w_in_ref, w_out_ref = refs[count : count + 2]
    base_ref = refs[count + 2]
    sends = refs[count + 3 : 2 * count + 2]
    normed_ref, filled_ref, acc_ref = refs[2 * count + 2 :]
    me = lax.axis_index("tp")
    mask_token = mtok_ref[...].astype(F32)[None, :]
    gain = gain_ref[...][None, :]
    for k in range(count):
        flag = flag_ref[k * rows : (k + 1) * rows, 0:1]
        values = jnp.where(flag > 0.5, mask_token, toks[k][0:rows, :].astype(F32))
        mean = jnp.mean(values, axis=1, keepdims=True)
        cent = values - mean
        var = jnp.mean(cent * cent, axis=1, keepdims=True)
        normed = cent * lax.rsqrt(var + 1e-05) * gain
        normed_ref[k * rows : (k + 1) * rows, :] = normed.astype(BF)
        filled_ref[k * rows : (k + 1) * rows, :] = values

    hidden_size = w_in_ref.shape[1]
    for at in range(0, hidden_size, chunk):
        pre = jnp.dot(normed_ref[...], w_in_ref[:, at : at + chunk], preferred_element_type=F32)
        pre = pre + bin_ref[at : at + chunk][None, :]
        hidden = (0.5 * pre * (1.0 + lax.erf(pre * math.sqrt(0.5)))).astype(BF)
        part = jnp.dot(hidden, w_out_ref[at : at + chunk, :], preferred_element_type=F32)
        if at == 0:
            acc_ref[...] = part
        else:
            acc_ref[...] += part

    bout = bout_ref[...][None, :]
    for k in range(count):
        parts = [(pl.ds(k * rows, rows), 0, rows)]
        if count == 2:
            low = lax.rem(me + k, count) == 0
            start = ((k + 1) % 2) * rows + jnp.where(low, 0, rows - BX)
            parts.append((pl.ds(pl.multiple_of(start, BX), BX), rows, BX))
        else:
            parts.append((pl.ds(((k - 1) % count) * rows + rows - BX, BX), rows, BX))
            parts.append((pl.ds(((k + 1) % count) * rows, BX), rows + BX, BX))
        for src, dst, size in parts:
            if k == 0:
                base_ref[dst : dst + size, :] = acc_ref[src, :] + filled_ref[src, :] + bout
            else:
                sends[k - 1][dst : dst + size, :] = acc_ref[src, :].astype(BF)


def mlp(tokens, peers, flags, mask_token, norm_gain, w_in, b_in, w_out, b_out):
    count = len(peers) + 1
    rows, width = tokens.shape
    hidden = w_in.shape[1]
    chunk = next(c for c in (256, 128, hidden) if hidden % c == 0)
    total = rows + (1 if count == 2 else 2) * BX
    outs = [jax.ShapeDtypeStruct((total, width), F32)] + [
        jax.ShapeDtypeStruct((total, width), BF) for _ in peers
    ]
    return pl.pallas_call(
        functools.partial(mlp_kernel, count, rows, chunk),
        in_specs=[in_vmem() for _ in range(8 + len(peers))],
        out_specs=[in_vmem() for _ in outs],
        out_shape=outs,
        scratch_shapes=[
            pltpu.VMEM((count * rows, width), BF),
            pltpu.VMEM((count * rows, width), F32),
            pltpu.VMEM((count * rows, width), F32),
        ],
        compiler_params=pltpu.CompilerParams(vmem_limit_bytes=16 * MIB),
        cost_estimate=pl.CostEstimate(
            flops=4 * count * rows * width * hidden,
            bytes_accessed=4 * width * hidden,
            transcendentals=count * rows * hidden,
        ),
        name="mlp",
    )(flags, mask_token, norm_gain, b_out, b_in, tokens, *peers, w_in, w_out)


def up_kernel(count, rows, arrived, first, base_ref, *refs):
    recvs = refs[:arrived]
    edges = refs[arrived : arrived + (1 if count == 2 else 2)]
    w_ref, bup_ref, skip_ref, outer_ref, inner_ref, sent_ref, bott_ref, wide_ref = refs[
        arrived + len(edges) :
    ]
    core = lax.rem(lax.axis_index("slab"), 2)
    me = lax.axis_index("tp")
    channels = bup_ref.shape[0]
    y_rows = rows // BX
    last = outer_ref.shape[0] - 1
    bias = bup_ref[...][None, :]

    total = base_ref[...]
    for r in recvs:
        total = total + r[...].astype(F32)
    bott_ref[...] = total.astype(BF)
    size = total.shape[0]

    for out_ref, b in [(ref, b) for ref in (outer_ref, inner_ref) for b in range(2)]:
        a = core if out_ref is outer_ref else 1 - core
        mine = pl.ds(pl.multiple_of(a * channels, 128), channels)
        start = pl.multiple_of((4 * a + 2 * b) * channels, 128)
        up = jnp.dot(bott_ref[...], w_ref[:, pl.ds(start, 2 * channels)], preferred_element_type=F32)
        for c in range(2):
            for l in range(0, channels, 128):
                wide_ref[b, l // 128, pl.ds(c, size, stride=2), :] = up[
                    :, c * channels + l : c * channels + l + 128
                ]

        def fine_row(at, b=b):
            return jnp.concatenate(
                [
                    wide_ref[b, l // 128, at * 2 * BX : (at + 1) * 2 * BX, :]
                    for l in range(0, channels, 128)
                ],
                axis=1,
            )

        for y in range(y_rows):
            row = fine_row(y) + bias + skip_ref[a, 2 * y + b].astype(F32)
            out_ref[1 + 2 * y + b] = row.astype(BF)
        if count == 2:
            value = fine_row(y_rows) + bias + edges[0][first:, mine].astype(F32)
            used = me == b
            out_ref[last if b == 0 else 0] = jnp.where(used, value, 0.0).astype(BF)
        else:
            slot = 1 - b
            ok = (me > 0) if slot == 0 else (me < count - 1)
            value = fine_row(y_rows + slot) + bias + edges[slot][first:, mine].astype(F32)
            out_ref[0 if slot == 0 else last] = jnp.where(ok, value, 0.0).astype(BF)
    if count == 2:
        sent_ref[...] = outer_ref[pl.ds(1 - me, last)]
    else:
        sent_ref[...] = outer_ref[...]


def upsample(count, rows, first, base, recvs, edges, w_up, b_up, skip):
    channels = b_up.shape[0]
    y_len, x_len = skip.shape[1:3]
    total, width = base.shape
    return pl.pallas_call(
        functools.partial(up_kernel, count, rows, len(recvs), first),
        in_specs=[in_vmem() for _ in range(4 + len(recvs) + len(edges))],
        out_specs=[in_vmem()] * 3,
        out_shape=[
            jax.ShapeDtypeStruct((y_len + n, x_len, channels), BF) for n in (2, 2, 1 if count == 2 else 2)
        ],
        scratch_shapes=[
            pltpu.VMEM((total, width), BF),
            pltpu.VMEM((2, channels // 128, 2 * total, 128), F32),
        ],
        compiler_params=pltpu.CompilerParams(vmem_limit_bytes=16 * MIB),
        cost_estimate=pl.CostEstimate(
            flops=16 * total * width * channels,
            bytes_accessed=2 * total * width,
            transcendentals=0,
        ),
        name="upsample",
    )(base, *recvs, *edges, w_up, b_up, skip)


def shifted_sum(sums, x_len):
    size, channels = sums.shape[0], sums.shape[1] // 3
    at_x = lax.rem(lax.broadcasted_iota(jnp.int32, (size, 1), 0), x_len)
    left, mid, right = (sums[:, i * channels : (i + 1) * channels] for i in range(3))
    left = jnp.where(at_x == 0, 0.0, pltpu.roll(left, 1, 0))
    right = jnp.where(at_x == x_len - 1, 0.0, pltpu.roll(right, size - 1, 0))
    return left + mid + right


def taps_dot(x_ref, w_ref, windows, y_len):
    x_len, channels = x_ref.shape[-2:]
    size = y_len * x_len
    rhs = [
        jnp.concatenate([w_ref[9 * dz + 3 * dy + dx] for dx in range(3)], axis=1)
        for _, dz, dy in windows
    ]
    lhs = [x_ref[plane, dy : dy + y_len].reshape(size, channels) for plane, _, dy in windows]
    return jnp.dot(
        jnp.concatenate(lhs, axis=1), jnp.concatenate(rhs, axis=0), preferred_element_type=F32
    )


def finish(total, bias_ref, shape):
    total = total + bias_ref[...][None, :]
    return jnp.where(total > 0, total, 0.01 * total).astype(BF).reshape(shape)


def main_kernel(units, chip_of, *refs):
    planes = refs[:3]
    count = sum(len(unit) - 1 for unit in units)
    pieces = [(step, *(refs[3 + n] for n in rest)) for step, *rest in units]
    bias_ref, out_ref, rest_ref, w_ref, x_ref, acc_ref, sem = refs[3 + count :]
    slab = lax.axis_index("slab")
    core = lax.rem(slab, 2)
    copies = []
    for n, plane in enumerate(planes):
        at = jnp.where(core == 0, n, 2 - n)
        copies.append(pltpu.make_async_copy(plane, x_ref.at[at], sem.at[n]))
    for copy in copies:
        copy.start()

    def assemble(windows):
        for step, *shards in pieces:
            for tap in [9 * dz + 3 * dy + dx for _, dz, dy in windows for dx in range(3)]:
                if len(shards) == 1:
                    w_ref[tap] = shards[0][tap]
                    continue
                a, b = (shard[tap] for shard in shards)
                band = a.shape[0] + b.shape[0]
                at = pl.multiple_of(chip_of(slab, step) * band, 16)
                w_ref[tap, pl.ds(at, band), :] = jnp.concatenate(
                    [jnp.where(core == 0, a, b), jnp.where(core == 0, b, a)], axis=0
                )

    y_len, x_len = out_ref.shape[:2]
    windows = [(dz, dz, dy) for dz in range(3) for dy in range(3)]
    assemble(windows[:4])
    for copy in copies:
        copy.wait()
    acc_ref[...] = taps_dot(x_ref, w_ref, windows[:4], y_len)
    assemble(windows[4:])
    sums = acc_ref[...] + taps_dot(x_ref, w_ref, windows[4:], y_len)
    out_ref[...] = finish(shifted_sum(sums, x_len), bias_ref, out_ref.shape)
    windows = [(core + i, 1 - core + i, dy) for i in range(2) for dy in range(3)]
    rest_ref[...] = shifted_sum(taps_dot(x_ref, w_ref, windows, y_len), x_len)


def last_kernel(count, beyond_ref, rest_ref, inner_ref, w_ref, bias_ref, out_ref, x_ref, sem):
    core = lax.rem(lax.axis_index("slab"), 2)
    me = lax.axis_index("tp")
    y_len, x_len = out_ref.shape[1:3]
    if count == 2:
        copy = pltpu.make_async_copy(beyond_ref, x_ref.at[0, pl.ds(1 - me, y_len + 1)], sem)
    else:
        copy = pltpu.make_async_copy(beyond_ref, x_ref.at[0], sem)
    copy.start()
    if count == 2:
        outside = jnp.where(me == 0, 0, y_len + 1)
        x_ref[0, outside] = jnp.zeros(x_ref.shape[2:], BF)
    out_ref[1 - core] = inner_ref[...]
    copy.wait()
    windows = [(0, 2 * core, dy) for dy in range(3)]
    total = rest_ref[...] + shifted_sum(taps_dot(x_ref, w_ref, windows, y_len), x_len)
    out_ref[core] = finish(total, bias_ref, inner_ref.shape)


def convolve(count, planes, units, chip_of, b_conv, y_len):
    x_len, channels = planes[1].shape[1:]
    size = y_len * x_len
    pieces = [piece for unit in units for piece in unit[1:]]
    numbered = iter(range(len(pieces)))
    marks = [(step, *(next(numbered) for _ in rest)) for step, *rest in units]
    plane = jax.ShapeDtypeStruct((y_len, x_len, channels), BF)

    def cost(windows):
        return pl.CostEstimate(
            flops=2 * size * windows * 3 * channels * channels,
            bytes_accessed=windows * 3 * channels * channels * 2,
            transcendentals=0,
        )

    inner, rest, weights = pl.pallas_call(
        functools.partial(main_kernel, marks, chip_of),
        in_specs=[pl.BlockSpec(memory_space=pl.ANY)] * 3 + [in_vmem() for _ in [*pieces, b_conv]],
        out_specs=[in_vmem()] * 3,
        out_shape=[
            plane,
            jax.ShapeDtypeStruct((size, channels), F32),
            jax.ShapeDtypeStruct((27, channels, channels), BF),
        ],
        scratch_shapes=[
            pltpu.VMEM((3, y_len + 2, x_len, channels), BF),
            pltpu.VMEM((size, 3 * channels), F32),
            pltpu.SemaphoreType.DMA((3,)),
        ],
        compiler_params=pltpu.CompilerParams(vmem_limit_bytes=30 * MIB),
        cost_estimate=cost(15),
        name="conv_main",
    )(*planes[1:], *pieces, b_conv)
    return pl.pallas_call(
        functools.partial(last_kernel, count),
        in_specs=[pl.BlockSpec(memory_space=pl.ANY)] + [in_vmem()] * 4,
        out_specs=in_vmem(),
        out_shape=jax.ShapeDtypeStruct((2, *plane.shape), BF),
        scratch_shapes=[
            pltpu.VMEM((1, y_len + 2, x_len, channels), BF),
            pltpu.SemaphoreType.DMA(()),
        ],
        compiler_params=pltpu.CompilerParams(vmem_limit_bytes=20 * MIB),
        cost_estimate=cost(3),
        name="conv_last",
    )(planes[0], rest, inner, weights, b_conv)


def gather_weights(w_conv, slabs, planes):
    chips = slabs // 2
    if chips % 2 or (2 * w_conv.shape[1]) % 16:
        whole = lax.all_gather(w_conv, "slab", axis=1, tiled=True)
        return [(0, whole)], None
    order = list(range(0, chips, 2)) + list(range(chips - 1, 0, -2))
    mates = [(s, s ^ 1) for s in range(slabs)]
    ring = []
    for at in range(chips):
        ring.append((2 * order[at], 2 * order[(at + 1) % chips]))
        ring.append((2 * order[at] + 1, 2 * order[(at - 1) % chips] + 1))

    def chip_of(slab, step):
        chip, sign = slab // 2, 1 - 2 * lax.rem(slab, 2)
        here = jnp.where(lax.rem(chip, 2) == 0, chip // 2, chips - 1 - chip // 2)
        at = lax.rem(here - sign * step + 2 * chips, chips)
        return jnp.where(2 * at < chips, 2 * at, 2 * (chips - 1 - at) + 1)

    pp = lax.ppermute

    def after(x, *others):
        return lax.optimization_barrier((x, others))[0]

    last = chips // 2
    a = pp(w_conv, "slab", ring)
    b = pp(w_conv, "slab", mates)
    units = [(0, w_conv, b)]
    for k in range(1, last):
        late = k == last - 1
        a_mate = pp(after(a, planes[3]) if late else a, "slab", mates)
        b = pp(b, "slab", ring)
        b_mate = pp(after(b, planes[3]) if late else b, "slab", mates)
        units += [(k, a, b), (-k, b_mate, a_mate)]
        a = pp(a, "slab", ring)
    units.append((last, a, pp(after(a, planes[3], b_mate), "slab", mates)))
    return units, chip_of


def on_device(
    tokens,
    mask_index,
    mask_token,
    norm_gain,
    w_in,
    b_in,
    w_out,
    b_out,
    w_up,
    b_up,
    skip,
    w_conv,
    b_conv,
):
    count = lax.axis_size("tp")
    slabs = lax.axis_size("slab")
    me = lax.axis_index("tp")
    rows, width = tokens.shape
    y_len, x_len, channels = skip.shape[1:]

    def from_peer(k):
        return [((i + k) % count, i) for i in range(count)]

    if count == 2:
        edge = lax.dynamic_index_in_dim(skip, jnp.where(me == 0, y_len - 1, 0), axis=1, keepdims=False)
        packed = jnp.concatenate([tokens, jnp.concatenate([edge[0], edge[1]], axis=1)], axis=0)
        packed = lax.ppermute(packed, "tp", from_peer(1))
        peers = [packed]
        edges, first = [packed], rows
    else:
        peers = [lax.ppermute(tokens, "tp", from_peer(k)) for k in range(1, count)]
        low, high = (jnp.concatenate([skip[0, y], skip[1, y]], axis=1) for y in (y_len - 1, 0))
        edges = [
            lax.ppermute(low, "tp", [(i, i + 1) for i in range(count - 1)]),
            lax.ppermute(high, "tp", [(i + 1, i) for i in range(count - 1)]),
        ]
        first = 0

    base, *sends = mlp(tokens, peers, mask_of(count, rows, mask_index), mask_token, norm_gain, w_in, b_in, w_out, b_out)
    recvs = [
        lax.ppermute(s, "tp", [(i, (i + k) % count) for i in range(count)])
        for k, s in enumerate(sends, start=1)
    ]
    outer, inner, sent = upsample(count, rows, first, base, recvs, edges, w_up, b_up, skip)
    pairs = [(s, s + 1) for s in range(1, slabs - 1, 2)]
    beyond = lax.ppermute(sent, "slab", pairs + [(t, s) for s, t in pairs])
    mates = lax.ppermute(inner, "slab", [(s, s ^ 1) for s in range(slabs)])
    planes = [beyond, outer, inner, mates]
    units, chip_of = gather_weights(w_conv, slabs, planes)
    return convolve(count, planes, units, chip_of, b_conv, y_len)


def solution(mesh):
    in_specs = (
        P(("slab", "tp"), None),
        P(),
        P(),
        P(),
        P(None, "tp"),
        P("tp"),
        P("tp", None),
        P(),
        P(),
        P(),
        P("slab", "tp", None, None),
        P(None, "slab", None),
        P(),
    )
    out_specs = P("slab", "tp", None, None)
    return jax.shard_map(
        on_device, mesh=mesh, in_specs=in_specs, out_specs=out_specs, check_vma=False
    )
```

```python
import functools
import math

import jax
import jax.numpy as jnp
from jax import lax
from jax.experimental import pallas as pl
from jax.experimental.pallas import tpu as pltpu
from jax.sharding import PartitionSpec as P

BF = jnp.bfloat16
F32 = jnp.float32
BX = 32
MIB = 1024 * 1024
FLAG_FLOPS = 6 * 10**9


def in_vmem(*_):
    return pl.BlockSpec(memory_space=pltpu.VMEM)


def in_smem(*_):
    return pl.BlockSpec(memory_space=pltpu.SMEM)


def mask_kernel(count, rows, mask_ref, flag_ref):
    me = lax.axis_index("tp")
    plane = lax.axis_index("slab") * (count * rows)
    index = mask_ref[...][None, :]
    for k in range(count):
        first = plane + lax.rem(me + k, count) * rows
        ids = lax.broadcasted_iota(jnp.int32, (rows, 1), 0) + first
        hit = jnp.max(jnp.where(index == ids, 1.0, 0.0), axis=1, keepdims=True)
        flag_ref[k * rows : (k + 1) * rows, :] = jnp.broadcast_to(hit, (rows, flag_ref.shape[1]))


def mask_of(count, rows, mask_index):
    return pl.pallas_call(
        functools.partial(mask_kernel, count, rows),
        in_specs=[in_vmem()],
        out_specs=in_vmem(),
        out_shape=jax.ShapeDtypeStruct((count * rows, 128), F32),
        compiler_params=pltpu.CompilerParams(vmem_limit_bytes=4 * MIB),
        cost_estimate=pl.CostEstimate(flops=FLAG_FLOPS, bytes_accessed=4 * MIB, transcendentals=0),
        name="mask",
    )(mask_index)


def mlp_kernel(count, rows, chunk, flag_ref, mtok_ref, gain_ref, bout_ref, bin_ref, *refs):
    toks = refs[:count]
    w_in_ref, w_out_ref = refs[count : count + 2]
    base_ref = refs[count + 2]
    sends = refs[count + 3 : 2 * count + 2]
    normed_ref, filled_ref, acc_ref = refs[2 * count + 2 :]
    me = lax.axis_index("tp")
    mask_token = mtok_ref[...].astype(F32)[None, :]
    gain = gain_ref[...][None, :]
    for k in range(count):
        flag = flag_ref[k * rows : (k + 1) * rows, 0:1]
        values = jnp.where(flag > 0.5, mask_token, toks[k][0:rows, :].astype(F32))
        mean = jnp.mean(values, axis=1, keepdims=True)
        cent = values - mean
        var = jnp.mean(cent * cent, axis=1, keepdims=True)
        normed = cent * lax.rsqrt(var + 1e-05) * gain
        normed_ref[k * rows : (k + 1) * rows, :] = normed.astype(BF)
        filled_ref[k * rows : (k + 1) * rows, :] = values

    hidden_size = w_in_ref.shape[1]
    for at in range(0, hidden_size, chunk):
        pre = jnp.dot(normed_ref[...], w_in_ref[:, at : at + chunk], preferred_element_type=F32)
        pre = pre + bin_ref[at : at + chunk][None, :]
        hidden = (0.5 * pre * (1.0 + lax.erf(pre * math.sqrt(0.5)))).astype(BF)
        part = jnp.dot(hidden, w_out_ref[at : at + chunk, :], preferred_element_type=F32)
        if at == 0:
            acc_ref[...] = part
        else:
            acc_ref[...] += part

    bout = bout_ref[...][None, :]
    for k in range(count):
        parts = [(pl.ds(k * rows, rows), 0, rows)]
        if count == 2:
            low = lax.rem(me + k, count) == 0
            start = ((k + 1) % 2) * rows + jnp.where(low, 0, rows - BX)
            parts.append((pl.ds(pl.multiple_of(start, BX), BX), rows, BX))
        else:
            parts.append((pl.ds(((k - 1) % count) * rows + rows - BX, BX), rows, BX))
            parts.append((pl.ds(((k + 1) % count) * rows, BX), rows + BX, BX))
        for src, dst, size in parts:
            if k == 0:
                base_ref[dst : dst + size, :] = acc_ref[src, :] + filled_ref[src, :] + bout
            else:
                sends[k - 1][dst : dst + size, :] = acc_ref[src, :].astype(BF)


def mlp(tokens, peers, flags, mask_token, norm_gain, w_in, b_in, w_out, b_out):
    count = len(peers) + 1
    rows, width = tokens.shape
    hidden = w_in.shape[1]
    chunk = next(c for c in (256, 128, hidden) if hidden % c == 0)
    total = rows + (1 if count == 2 else 2) * BX
    outs = [jax.ShapeDtypeStruct((total, width), F32)] + [
        jax.ShapeDtypeStruct((total, width), BF) for _ in peers
    ]
    return pl.pallas_call(
        functools.partial(mlp_kernel, count, rows, chunk),
        in_specs=[in_vmem() for _ in range(8 + len(peers))],
        out_specs=[in_vmem() for _ in outs],
        out_shape=outs,
        scratch_shapes=[
            pltpu.VMEM((count * rows, width), BF),
            pltpu.VMEM((count * rows, width), F32),
            pltpu.VMEM((count * rows, width), F32),
        ],
        compiler_params=pltpu.CompilerParams(vmem_limit_bytes=16 * MIB),
        cost_estimate=pl.CostEstimate(
            flops=4 * count * rows * width * hidden,
            bytes_accessed=4 * width * hidden,
            transcendentals=count * rows * hidden,
        ),
        name="mlp",
    )(flags, mask_token, norm_gain, b_out, b_in, tokens, *peers, w_in, w_out)


def up_kernel(count, rows, arrived, first, base_ref, *refs):
    recvs = refs[:arrived]
    edges = refs[arrived : arrived + (1 if count == 2 else 2)]
    w_ref, bup_ref, skip_ref, outer_ref, inner_ref, sent_ref, bott_ref, wide_ref = refs[
        arrived + len(edges) :
    ]
    core = lax.rem(lax.axis_index("slab"), 2)
    me = lax.axis_index("tp")
    channels = bup_ref.shape[0]
    y_rows = rows // BX
    last = outer_ref.shape[0] - 1
    bias = bup_ref[...][None, :]

    total = base_ref[...]
    for r in recvs:
        total = total + r[...].astype(F32)
    bott_ref[...] = total.astype(BF)
    size = total.shape[0]

    for out_ref, b in [(ref, b) for ref in (outer_ref, inner_ref) for b in range(2)]:
        a = core if out_ref is outer_ref else 1 - core
        mine = pl.ds(pl.multiple_of(a * channels, 128), channels)
        start = pl.multiple_of((4 * a + 2 * b) * channels, 128)
        up = jnp.dot(bott_ref[...], w_ref[:, pl.ds(start, 2 * channels)], preferred_element_type=F32)
        for c in range(2):
            for l in range(0, channels, 128):
                wide_ref[b, l // 128, pl.ds(c, size, stride=2), :] = up[
                    :, c * channels + l : c * channels + l + 128
                ]

        def fine_row(at, b=b):
            return jnp.concatenate(
                [
                    wide_ref[b, l // 128, at * 2 * BX : (at + 1) * 2 * BX, :]
                    for l in range(0, channels, 128)
                ],
                axis=1,
            )

        for y in range(y_rows):
            row = fine_row(y) + bias + skip_ref[a, 2 * y + b].astype(F32)
            out_ref[1 + 2 * y + b] = row.astype(BF)
        if count == 2:
            value = fine_row(y_rows) + bias + edges[0][first:, mine].astype(F32)
            used = me == b
            out_ref[last if b == 0 else 0] = jnp.where(used, value, 0.0).astype(BF)
        else:
            slot = 1 - b
            ok = (me > 0) if slot == 0 else (me < count - 1)
            value = fine_row(y_rows + slot) + bias + edges[slot][first:, mine].astype(F32)
            out_ref[0 if slot == 0 else last] = jnp.where(ok, value, 0.0).astype(BF)
    if count == 2:
        sent_ref[...] = outer_ref[pl.ds(1 - me, last)]
    else:
        sent_ref[...] = outer_ref[...]


def upsample(count, rows, first, base, recvs, edges, w_up, b_up, skip):
    channels = b_up.shape[0]
    y_len, x_len = skip.shape[1:3]
    total, width = base.shape
    return pl.pallas_call(
        functools.partial(up_kernel, count, rows, len(recvs), first),
        in_specs=[in_vmem() for _ in range(4 + len(recvs) + len(edges))],
        out_specs=[in_vmem()] * 3,
        out_shape=[
            jax.ShapeDtypeStruct((y_len + n, x_len, channels), BF) for n in (2, 2, 1 if count == 2 else 2)
        ],
        scratch_shapes=[
            pltpu.VMEM((total, width), BF),
            pltpu.VMEM((2, channels // 128, 2 * total, 128), F32),
        ],
        compiler_params=pltpu.CompilerParams(vmem_limit_bytes=16 * MIB),
        cost_estimate=pl.CostEstimate(
            flops=16 * total * width * channels,
            bytes_accessed=2 * total * width,
            transcendentals=0,
        ),
        name="upsample",
    )(base, *recvs, *edges, w_up, b_up, skip)


def shifted_sum(sums, x_len):
    size, channels = sums.shape[0], sums.shape[1] // 3
    at_x = lax.rem(lax.broadcasted_iota(jnp.int32, (size, 1), 0), x_len)
    left, mid, right = (sums[:, i * channels : (i + 1) * channels] for i in range(3))
    left = jnp.where(at_x == 0, 0.0, pltpu.roll(left, 1, 0))
    right = jnp.where(at_x == x_len - 1, 0.0, pltpu.roll(right, size - 1, 0))
    return left + mid + right


def taps_dot(x_ref, w_ref, windows, y_len):
    x_len, channels = x_ref.shape[-2:]
    size = y_len * x_len
    rhs = [
        jnp.concatenate([w_ref[9 * dz + 3 * dy + dx] for dx in range(3)], axis=1)
        for _, dz, dy in windows
    ]
    lhs = [x_ref[plane, dy : dy + y_len].reshape(size, channels) for plane, _, dy in windows]
    return jnp.dot(
        jnp.concatenate(lhs, axis=1), jnp.concatenate(rhs, axis=0), preferred_element_type=F32
    )


def finish(total, bias_ref, shape):
    total = total + bias_ref[...][None, :]
    return jnp.where(total > 0, total, 0.01 * total).astype(BF).reshape(shape)


def main_kernel(units, chip_of, *refs):
    planes = refs[:3]
    count = sum(len(unit) - 1 for unit in units)
    pieces = [(step, *(refs[3 + n] for n in rest)) for step, *rest in units]
    bias_ref, out_ref, rest_ref, w_ref, x_ref, acc_ref, sem = refs[3 + count :]
    slab = lax.axis_index("slab")
    core = lax.rem(slab, 2)
    copies = []
    for n, plane in enumerate(planes):
        at = jnp.where(core == 0, n, 2 - n)
        copies.append(pltpu.make_async_copy(plane, x_ref.at[at], sem.at[n]))
    for copy in copies:
        copy.start()

    def assemble(windows):
        for step, *shards in pieces:
            for tap in [9 * dz + 3 * dy + dx for _, dz, dy in windows for dx in range(3)]:
                if len(shards) == 1:
                    w_ref[tap] = shards[0][tap]
                    continue
                a, b = (shard[tap] for shard in shards)
                band = a.shape[0] + b.shape[0]
                at = pl.multiple_of(chip_of(slab, step) * band, 16)
                w_ref[tap, pl.ds(at, band), :] = jnp.concatenate(
                    [jnp.where(core == 0, a, b), jnp.where(core == 0, b, a)], axis=0
                )

    y_len, x_len = out_ref.shape[:2]
    windows = [(dz, dz, dy) for dz in range(3) for dy in range(3)]
    assemble(windows[:4])
    for copy in copies:
        copy.wait()
    acc_ref[...] = taps_dot(x_ref, w_ref, windows[:4], y_len)
    assemble(windows[4:])
    sums = acc_ref[...] + taps_dot(x_ref, w_ref, windows[4:], y_len)
    out_ref[...] = finish(shifted_sum(sums, x_len), bias_ref, out_ref.shape)
    windows = [(core + i, 1 - core + i, dy) for i in range(2) for dy in range(3)]
    rest_ref[...] = shifted_sum(taps_dot(x_ref, w_ref, windows, y_len), x_len)


def last_kernel(count, beyond_ref, rest_ref, inner_ref, w_ref, bias_ref, out_ref, x_ref, sem):
    core = lax.rem(lax.axis_index("slab"), 2)
    me = lax.axis_index("tp")
    y_len, x_len = out_ref.shape[1:3]
    if count == 2:
        copy = pltpu.make_async_copy(beyond_ref, x_ref.at[0, pl.ds(1 - me, y_len + 1)], sem)
    else:
        copy = pltpu.make_async_copy(beyond_ref, x_ref.at[0], sem)
    copy.start()
    if count == 2:
        outside = jnp.where(me == 0, 0, y_len + 1)
        x_ref[0, outside] = jnp.zeros(x_ref.shape[2:], BF)
    out_ref[1 - core] = inner_ref[...]
    copy.wait()
    windows = [(0, 2 * core, dy) for dy in range(3)]
    total = rest_ref[...] + shifted_sum(taps_dot(x_ref, w_ref, windows, y_len), x_len)
    out_ref[core] = finish(total, bias_ref, inner_ref.shape)


def convolve(count, planes, units, chip_of, b_conv, y_len):
    x_len, channels = planes[1].shape[1:]
    size = y_len * x_len
    pieces = [piece for unit in units for piece in unit[1:]]
    numbered = iter(range(len(pieces)))
    marks = [(step, *(next(numbered) for _ in rest)) for step, *rest in units]
    plane = jax.ShapeDtypeStruct((y_len, x_len, channels), BF)

    def cost(windows):
        return pl.CostEstimate(
            flops=2 * size * windows * 3 * channels * channels,
            bytes_accessed=windows * 3 * channels * channels * 2,
            transcendentals=0,
        )

    inner, rest, weights = pl.pallas_call(
        functools.partial(main_kernel, marks, chip_of),
        in_specs=[pl.BlockSpec(memory_space=pl.ANY)] * 3 + [in_vmem() for _ in [*pieces, b_conv]],
        out_specs=[in_vmem()] * 3,
        out_shape=[
            plane,
            jax.ShapeDtypeStruct((size, channels), F32),
            jax.ShapeDtypeStruct((27, channels, channels), BF),
        ],
        scratch_shapes=[
            pltpu.VMEM((3, y_len + 2, x_len, channels), BF),
            pltpu.VMEM((size, 3 * channels), F32),
            pltpu.SemaphoreType.DMA((3,)),
        ],
        compiler_params=pltpu.CompilerParams(vmem_limit_bytes=30 * MIB),
        cost_estimate=cost(15),
        name="conv_main",
    )(*planes[1:], *pieces, b_conv)
    return pl.pallas_call(
        functools.partial(last_kernel, count),
        in_specs=[pl.BlockSpec(memory_space=pl.ANY)] + [in_vmem()] * 4,
        out_specs=in_vmem(),
        out_shape=jax.ShapeDtypeStruct((2, *plane.shape), BF),
        scratch_shapes=[
            pltpu.VMEM((1, y_len + 2, x_len, channels), BF),
            pltpu.SemaphoreType.DMA(()),
        ],
        compiler_params=pltpu.CompilerParams(vmem_limit_bytes=20 * MIB),
        cost_estimate=cost(3),
        name="conv_last",
    )(planes[0], rest, inner, weights, b_conv)


def gather_weights(w_conv, slabs, planes):
    chips = slabs // 2
    if chips % 2 or (2 * w_conv.shape[1]) % 16:
        whole = lax.all_gather(w_conv, "slab", axis=1, tiled=True)
        return [(0, whole)], None
    order = list(range(0, chips, 2)) + list(range(chips - 1, 0, -2))
    mates = [(s, s ^ 1) for s in range(slabs)]
    ring = []
    for at in range(chips):
        ring.append((2 * order[at], 2 * order[(at + 1) % chips]))
        ring.append((2 * order[at] + 1, 2 * order[(at - 1) % chips] + 1))

    def chip_of(slab, step):
        chip, sign = slab // 2, 1 - 2 * lax.rem(slab, 2)
        here = jnp.where(lax.rem(chip, 2) == 0, chip // 2, chips - 1 - chip // 2)
        at = lax.rem(here - sign * step + 2 * chips, chips)
        return jnp.where(2 * at < chips, 2 * at, 2 * (chips - 1 - at) + 1)

    pp = lax.ppermute

    def after(x, *others):
        return lax.optimization_barrier((x, others))[0]

    last = chips // 2
    a = pp(w_conv, "slab", ring)
    b = pp(w_conv, "slab", mates)
    units, met = [(0, w_conv, b)], []
    for k in range(1, last):
        late = k == last - 1
        a_mate = pp(after(a, planes[3]) if late else a, "slab", mates)
        b = pp(b, "slab", ring)
        b_mate = pp(after(b, planes[3]) if late else b, "slab", mates)
        units += [(k, a, b), (-k, b_mate, a_mate)]
        met = [*met[-1:], b_mate]
        a = pp(a, "slab", ring)
    units.append((last, a, pp(after(a, planes[3], *met), "slab", mates)))
    return units, chip_of


def on_device(
    tokens,
    mask_index,
    mask_token,
    norm_gain,
    w_in,
    b_in,
    w_out,
    b_out,
    w_up,
    b_up,
    skip,
    w_conv,
    b_conv,
):
    count = lax.axis_size("tp")
    slabs = lax.axis_size("slab")
    me = lax.axis_index("tp")
    rows, width = tokens.shape
    y_len, x_len, channels = skip.shape[1:]

    def from_peer(k):
        return [((i + k) % count, i) for i in range(count)]

    if count == 2:
        edge = lax.dynamic_index_in_dim(skip, jnp.where(me == 0, y_len - 1, 0), axis=1, keepdims=False)
        packed = jnp.concatenate([tokens, jnp.concatenate([edge[0], edge[1]], axis=1)], axis=0)
        packed = lax.ppermute(packed, "tp", from_peer(1))
        peers = [packed]
        edges, first = [packed], rows
    else:
        peers = [lax.ppermute(tokens, "tp", from_peer(k)) for k in range(1, count)]
        low, high = (jnp.concatenate([skip[0, y], skip[1, y]], axis=1) for y in (y_len - 1, 0))
        edges = [
            lax.ppermute(low, "tp", [(i, i + 1) for i in range(count - 1)]),
            lax.ppermute(high, "tp", [(i + 1, i) for i in range(count - 1)]),
        ]
        first = 0

    base, *sends = mlp(tokens, peers, mask_of(count, rows, mask_index), mask_token, norm_gain, w_in, b_in, w_out, b_out)
    recvs = [
        lax.ppermute(s, "tp", [(i, (i + k) % count) for i in range(count)])
        for k, s in enumerate(sends, start=1)
    ]
    outer, inner, sent = upsample(count, rows, first, base, recvs, edges, w_up, b_up, skip)
    pairs = [(s, s + 1) for s in range(1, slabs - 1, 2)]
    beyond = lax.ppermute(sent, "slab", pairs + [(t, s) for s, t in pairs])
    mates = lax.ppermute(inner, "slab", [(s, s ^ 1) for s in range(slabs)])
    planes = [beyond, outer, inner, mates]
    units, chip_of = gather_weights(w_conv, slabs, planes)
    return convolve(count, planes, units, chip_of, b_conv, y_len)


def solution(mesh):
    in_specs = (
        P(("slab", "tp"), None),
        P(),
        P(),
        P(),
        P(None, "tp"),
        P("tp"),
        P("tp", None),
        P(),
        P(),
        P(),
        P("slab", "tp", None, None),
        P(None, "slab", None),
        P(),
    )
    out_specs = P("slab", "tp", None, None)
    return jax.shard_map(
        on_device, mesh=mesh, in_specs=in_specs, out_specs=out_specs, check_vma=False
    )
```
